512 devices in a mesh: dp: 64 (over x, z), tensor: 8 (over y, core).
Axes of the slice: x: 4, y: 4, z: 16, core: 2. Of those that a mesh axis runs over, the one named last changes fastest.
Arguments:
- tiles: bfloat16 [1024, 24, 1280], P('dp', 'tensor'), may hold values from -6 to 6
- window_ids: int32 [1024, 24], P('dp', 'tensor'), may hold values from 0 to 3, never falling along the last dimension, each value on 1 to 12 neighbouring positions
- counts: int32 [64], replicated, may hold values from 0 to 16, as said below
- ln_gain: bfloat16 [1280], replicated, may hold values from 0.099609375 to 1.8984375
- ln_bias: bfloat16 [1280], replicated, may hold values from -3 to 3
- qkv_weight: bfloat16 [3, 1280, 1280], P(None, None, 'tensor'), may hold values from -0.15625 to 0.15625
- qkv_bias: bfloat16 [3, 1280], P(None, 'tensor'), may hold values from -3 to 3
- proj_weight: bfloat16 [1280, 1280], P('tensor'), may hold values from -0.15625 to 0.15625
- proj_bias: bfloat16 [1280], replicated, may hold values from -3 to 3
- mlp_gain: bfloat16 [1280], replicated, may hold values from 0.099609375 to 1.8984375
- mlp_bias: bfloat16 [1280], replicated, may hold values from -3 to 3
- fc1_weight: bfloat16 [1280, 2560], P(None, 'tensor'), may hold values from -0.15625 to 0.15625
- fc1_bias: bfloat16 [2560], P('tensor'), may hold values from -3 to 3
- fc2_weight: bfloat16 [2560, 1280], P('tensor'), may hold values from -0.125 to 0.125
- fc2_bias: bfloat16 [1280], replicated, may hold values from -3 to 3
Outputs:
- encoded: bfloat16 [1024, 24, 1280], P('dp', 'tensor')
The draws below stay inside these ranges and needn't reach their ends.
Inputs may be any that keep to these rules, and one draw needn't show every extreme that they name: `counts`: for each device d below 32, exactly one of devices d and d + 32 owns tiles, and it owns more than 8; device 0 owns 16, and device 64 / 2 - 1 owns tiles.
All inputs are finite; a program needn't handle non-finite values.
Results may differ from the reference program's by a relative error of at most 0.02.
Values may be sent and summed in bfloat16 or wider, within the bound.
A program may use at most 64 MiB of HBM per device.

```python
import math
import jax
import jax.numpy as jnp
import numpy as np
from jax import lax

D = 1280
HEADS = 16
HEAD_DIM = 80
MLP = 2560
TILE = 24
PROC = 8
SLOTS = 16
TILES_ALL = 1024
N_DP = 64
N_TENSOR = 8


def draw_counts(key, part):
    key = jax.random.fold_in(key, 11)
    half_peers = N_DP // 2
    key_side, key_load = jax.random.split(key)
    side = jax.random.randint(key_side, (half_peers,), 0, 2).astype(jnp.int32)
    side = side.at[0].set(0)
    side = side.at[half_peers - 1].set(0)
    senders = jnp.arange(half_peers, dtype=jnp.int32) + side * half_peers
    lowest = max(1, PROC - PROC // 8)
    overflow = jax.random.randint(key_load, (half_peers,), lowest, PROC + 1).astype(jnp.int32)
    overflow = overflow.at[0].set(PROC)
    return jnp.zeros((N_DP,), jnp.int32).at[senders].set(PROC + overflow)


def shard_levels(rng, extent, pieces, smallest, top_value):
    level = 1.0
    for dim, parts in pieces:
        draws = jax.random.uniform(jax.random.fold_in(jax.random.fold_in(rng, 6), dim), (parts,), jnp.float32, smallest / len(pieces), top_value / len(pieces))
        level = level * jnp.repeat(jnp.exp(draws), extent[dim] // parts).reshape((-1,) + (1,) * (len(extent) - 1 - dim))
    return level


def split_up(amount, total, reach, skew):
    portions = [(1 << 20) // math.isqrt(grade ** skew) + 1 for grade in range(2, amount + 1)]
    spare, given = total - reach - (amount - 1), [1] * (amount - 1)
    while spare > 0:
        candidates = [i for i in range(amount - 1) if given[i] < reach]
        pool, remaining = sum([portions[i] for i in candidates]), spare
        for i in candidates:
            more = min(reach - given[i], max(1, remaining * portions[i] // pool), spare)
            given[i] = given[i] + more
            spare = spare - more
    return np.array([reach] + given)


def uneven(key, count, total, limit, slope):
    if count == 2:
        one = jax.random.randint(key, (), max(1, total - limit), min(limit, total - 1) + 1)
        return jnp.stack([one, total - one])
    tallies = jnp.asarray(split_up(count, total, limit, slope), jnp.int32)
    couples = (count - 1) // 2
    donor, receiver = tallies[1:1 + 2 * couples:2], tallies[2:2 + 2 * couples:2]
    margin = jnp.minimum(donor - 1, limit - receiver)
    moved = jax.random.randint(jax.random.fold_in(key, 1), (couples,), 0, 1 << 20) % (margin + 1)
    tallies = tallies.at[1:1 + 2 * couples:2].set(donor - moved).at[2:2 + 2 * couples:2].set(receiver + moved)
    return tallies[jax.random.permutation(jax.random.fold_in(key, 2), count)]


def gaussian(stream_key, shape, scale, limit, cuts=(), held_as=jnp.bfloat16):
    values = jax.random.normal(stream_key, shape, jnp.float32) * scale
    if len(cuts) > 0:
        values = shard_levels(stream_key, shape, cuts, -0.22, 0.18) * values
    return jnp.clip(values, min=-limit, max=limit).astype(held_as)


def setup_inputs(seed: int = 0) -> dict:
    streams_of = jax.random.split(jax.random.key(seed), 16)
    tiles = gaussian(streams_of[0], (TILES_ALL, TILE, D), 1.0, 6.0, ((0, 64), (1, 8)))
    window_ids = jax.vmap(lambda own: jnp.searchsorted(jnp.cumsum(uneven(own, 4, TILE, TILE // 2, 2)), jnp.arange(TILE), side="right"))(jax.random.split(streams_of[1], TILES_ALL)).reshape((TILES_ALL, TILE)).astype(jnp.int32)
    counts = draw_counts(jax.random.fold_in(streams_of[15], 71), 0)
    ln_gain = jnp.clip(1.0 + 0.18 * jax.random.normal(streams_of[3], (D,), jnp.float32), 0.099609375, 1.8984375).astype(jnp.bfloat16)
    ln_bias = gaussian(streams_of[4], (D,), 0.3, 3.0)
    qkv_weight = gaussian(streams_of[5], (3, D, HEADS * HEAD_DIM), D ** -0.5, 0.15625, ((2, 8),))
    qkv_bias = gaussian(streams_of[6], (3, HEADS * HEAD_DIM), 0.5, 3.0, ((1, 8),))
    proj_weight = gaussian(streams_of[7], (HEADS * HEAD_DIM, D), (HEADS * HEAD_DIM) ** -0.5, 0.15625, ((0, 8),))
    proj_bias = gaussian(streams_of[8], (D,), 0.3, 3.0)
    mlp_gain = jnp.clip(1.0 + 0.18 * jax.random.normal(streams_of[9], (D,), jnp.float32), 0.099609375, 1.8984375).astype(jnp.bfloat16)
    mlp_bias = gaussian(streams_of[10], (D,), 0.3, 3.0)
    fc1_weight = gaussian(streams_of[11], (D, MLP), D ** -0.5, 0.15625, ((1, 8),))
    fc1_bias = gaussian(streams_of[12], (MLP,), 0.5, 3.0, ((0, 8),))
    fc2_weight = gaussian(streams_of[13], (MLP, D), MLP ** -0.5, 0.125, ((0, 8),))
    fc2_bias = gaussian(streams_of[14], (D,), 0.3, 3.0)
    return dict(tiles=tiles, window_ids=window_ids, counts=counts, ln_gain=ln_gain, ln_bias=ln_bias, qkv_weight=qkv_weight, qkv_bias=qkv_bias, proj_weight=proj_weight, proj_bias=proj_bias, mlp_gain=mlp_gain, mlp_bias=mlp_bias, fc1_weight=fc1_weight, fc1_bias=fc1_bias, fc2_weight=fc2_weight, fc2_bias=fc2_bias)


def layer_norm(widened, gain, shift):
    row_mean = lax.optimization_barrier(jnp.mean(widened, axis=-1, keepdims=True))
    centred = widened - row_mean
    variance = lax.optimization_barrier(jnp.mean(centred * centred, axis=-1, keepdims=True))
    normed = centred * lax.rsqrt(variance + 1e-06) * gain.astype(jnp.float32) + shift.astype(jnp.float32)
    return normed.astype(jnp.bfloat16)

def grouped_sum(left, right, group_width, row_total):
    summed_all = jnp.zeros((row_total, right.shape[1]), jnp.float32)
    for member in range(N_TENSOR):
        partial_value = jnp.dot(left[:, member * group_width:(member + 1) * group_width], right[member * group_width:(member + 1) * group_width], preferred_element_type=jnp.float32).astype(jnp.bfloat16)
        partial_value = lax.optimization_barrier(partial_value)
        summed_all = summed_all + partial_value.astype(jnp.float32)
    return summed_all

def encode_block(tile_rows, window_of, live_count, ln_gain, ln_bias, qkv_weight, qkv_bias, proj_weight, proj_bias, mlp_gain, mlp_bias, fc1_weight, fc1_bias, fc2_weight, fc2_bias):
    tile_count = tile_rows.shape[0]
    row_total = tile_count * TILE
    widened = tile_rows.astype(jnp.float32).reshape(row_total, D)
    normed = layer_norm(widened, ln_gain, ln_bias)
    width = HEADS * HEAD_DIM

    def project(which):
        values_out = jnp.dot(normed, qkv_weight[which], preferred_element_type=jnp.float32) + qkv_bias[which].astype(jnp.float32)
        return values_out.astype(jnp.bfloat16).reshape(tile_count, TILE, HEADS, HEAD_DIM)
    query = project(0)
    keys = project(1)
    values = project(2)
    scores = jnp.einsum('ntha,nsha->nhts', query.astype(jnp.float32), keys.astype(jnp.float32)) / jnp.sqrt(jnp.float32(HEAD_DIM))
    same_window = window_of[:, None, :, None] == window_of[:, None, None, :]
    weights = jnp.where(same_window, jnp.exp(scores), jnp.float32(0.0))
    attention = (weights / lax.optimization_barrier(jnp.sum(weights, axis=-1, keepdims=True))).astype(jnp.bfloat16)
    attended = jnp.einsum('nhts,nsha->ntha', attention.astype(jnp.float32), values.astype(jnp.float32))
    attended = attended.astype(jnp.bfloat16).reshape(row_total, width)
    head_total = grouped_sum(attended, proj_weight, width // N_TENSOR, row_total)
    mixed = (head_total + proj_bias.astype(jnp.float32) + widened).astype(jnp.bfloat16)
    normed2 = layer_norm(mixed.astype(jnp.float32), mlp_gain, mlp_bias)
    before = jnp.dot(normed2, fc1_weight, preferred_element_type=jnp.float32) + fc1_bias.astype(jnp.float32)
    hidden = (before * jax.nn.sigmoid(1.702 * before)).astype(jnp.bfloat16)
    ffn_total = grouped_sum(hidden, fc2_weight, MLP // N_TENSOR, row_total)
    encoded = mixed.astype(jnp.float32) + fc2_bias.astype(jnp.float32) + ffn_total
    encoded = encoded.astype(jnp.bfloat16).reshape(tile_count, TILE, D)
    live_slots = jnp.arange(tile_count, dtype=jnp.int32) < live_count
    return jnp.where(live_slots[:, None, None], encoded, jnp.zeros_like(encoded))

def reference(tiles, window_ids, counts, ln_gain, ln_bias, qkv_weight, qkv_bias, proj_weight, proj_bias, mlp_gain, mlp_bias, fc1_weight, fc1_bias, fc2_weight, fc2_bias):
    blocks = tiles.reshape(N_DP, SLOTS, TILE, D)
    windows = window_ids.reshape(N_DP, SLOTS, TILE)

    def encode_device(inputs):
        block, window_of, live_count = inputs
        return encode_block(block, window_of, live_count, ln_gain, ln_bias, qkv_weight, qkv_bias, proj_weight, proj_bias, mlp_gain, mlp_bias, fc1_weight, fc1_bias, fc2_weight, fc2_bias)
    encoded = lax.map(encode_device, (blocks, windows, counts))
    return encoded.reshape(TILES_ALL, TILE, D)
```

```python
import jax
import jax.numpy as jnp
from jax import lax
from jax.experimental import pallas as pl
from jax.experimental.pallas import tpu as pltpu
from jax.sharding import PartitionSpec as P

D = 1280
HEAD_DIM = 80
LANES = 128
WIDE = D + LANES
QUARTER = 16
ROWS = 24
CHIPS = 4
GROUP = CHIPS * ROWS
MESH = pl.DeviceIdType.MESH
F32 = jnp.float32
BF16 = jnp.bfloat16


def matmul(left, right):
    return jnp.dot(left, right, preferred_element_type=F32)


def matmul_t(left, right):
    return lax.dot_general(left, right, (((1,), (1,)), ((), ())), preferred_element_type=F32)


def normalize(rows, gain, shift):
    centred = rows - jnp.mean(rows, axis=-1, keepdims=True)
    variance = jnp.mean(centred * centred, axis=-1, keepdims=True)
    return (centred * lax.rsqrt(variance + 1e-06) * gain + shift).astype(BF16)


def iotas(shape):
    return (
        lax.broadcasted_iota(jnp.int32, shape, 0),
        lax.broadcasted_iota(jnp.int32, shape, 1),
    )


def one_hot(flags):
    return jnp.where(flags, 1.0, 0.0).astype(BF16)


def encode(
    counts,
    window,
    vectors,
    tiles,
    qkv_weight,
    proj_weight,
    fc1_weight,
    fc2_weight,
    out,
    vec,
    wqkv,
    wproj,
    wfc1,
    wfc2,
    tile_rows,
    quarter_out,
    quarter_in,
    normed_all,
    part_out,
    part_in,
    normed2_all,
    ffn_out,
    ffn_in,
    done_out,
    done_in,
    load_sem,
    weight_send,
    weight_recv,
    lend_send,
    lend_recv,
    ring_send,
    ring_recv,
    back_send,
    back_recv,
):
    d, t = lax.axis_index("dp"), lax.axis_index("tensor")
    y, c = t // 2, t % 2
    pd = (d + 32) % 64
    sib = y * 2 + (1 - c)
    around = [(d, ((y + k) % CHIPS) * 2 + c) for k in (2, 1, 3)]
    beside = [(d, sib), (pd, t), (pd, sib)]

    barrier = pltpu.get_barrier_semaphore()
    for peer in beside + around:
        pl.semaphore_signal(barrier, inc=1, device_id=peer, device_id_type=MESH)

    loads = [(tiles, tile_rows), (vectors, vec.at[c])]
    pushes = [(vectors, vec.at[c])]
    for which in range(3):
        for head in range(2):
            pair = (
                qkv_weight.at[which, pl.ds(head * HEAD_DIM, HEAD_DIM)],
                wqkv.at[c, which, head, pl.ds(0, HEAD_DIM)],
            )
            loads.append(pair)
            pushes.append(pair)
    for head in range(2):
        pair = (
            proj_weight.at[pl.ds(head * HEAD_DIM, HEAD_DIM)],
            wproj.at[c, head, pl.ds(0, HEAD_DIM)],
        )
        loads.append(pair)
        pushes.append(pair)
    for pair in ((fc1_weight, wfc1.at[c]), (fc2_weight, wfc2.at[c])):
        loads.append(pair)
        pushes.append(pair)
    started = []
    for i, (src, dst) in enumerate(loads):
        started.append(pltpu.make_async_copy(src, dst, load_sem.at[i]))
        started[-1].start()

    gap = jnp.zeros((LANES - HEAD_DIM, D), BF16)
    for core in range(2):
        for head in range(2):
            for which in range(3):
                wqkv[core, which, head, HEAD_DIM:] = gap
            wproj[core, head, HEAD_DIM:] = gap

    own_count = counts[d]
    pair_count = own_count + counts[pd]
    side = jnp.where(own_count > 0, 0, 1)

    row, col = iotas((16, 16))
    labels = []
    for token in range(3):
        picked = jnp.where(row == col, window[token : token + 1, :].astype(F32), 0.0)
        labels.append(jnp.sum(picked, axis=1, keepdims=True))
    labels = jnp.broadcast_to(jnp.concatenate(labels, axis=0), (48, LANES)).astype(BF16)
    row, col = iotas((64, 48))
    inner = row % QUARTER
    pick = one_hot((inner < 12) & (col == (inner // 4) * 16 + (row // QUARTER) * 4 + inner % 4))
    started[0].wait()
    features = tile_rows[...].reshape(48, D)
    quarters = matmul(pick, jnp.concatenate([features, labels], axis=1))
    quarter_out[...] = quarters.astype(BF16).reshape(4, QUARTER, WIDE)
    quarter_in[0, c] = quarter_out[c]

    pl.semaphore_wait(barrier, len(beside) + len(around))

    def remote(src, dst, sems, peer):
        copy = pltpu.make_async_remote_copy(
            src_ref=src,
            dst_ref=dst,
            send_sem=sems[0],
            recv_sem=sems[1],
            device_id=peer,
            device_id_type=MESH,
        )
        copy.start()
        return copy

    sent = []
    lends = []
    for i, (peer, block, where) in enumerate(
        (
            (beside[1], 2 + c, 1),
            (beside[2], 3 - c, 1),
            (beside[0], 1 - c, 0),
        )
    ):
        lends.append(
            remote(
                quarter_out.at[block],
                quarter_in.at[where, c],
                (lend_send.at[i], lend_recv.at[i]),
                peer,
            )
        )
    pushed = []
    for i, (src, dst) in enumerate(pushes):
        pushed.append(remote(src, dst, (weight_send.at[i], weight_recv.at[i]), beside[0]))
    sent += lends + pushed
    for copy in lends:
        copy.wait_recv()

    row, col = iotas((ROWS, 64))
    inner = col % QUARTER
    pick = one_hot(
        (inner < 12) & (col // 32 == side) & (row == ((col % 32) // QUARTER) * 12 + inner)
    )
    mine = matmul(pick, quarter_in[...].reshape(64, WIDE))
    rows_in = mine[:, :D]

    started[1].wait()

    def vector(i):
        return vec[c, i : i + 1, :].astype(F32)

    def spread(buffer, phase):
        copies = []
        for i, peer in enumerate(around):
            copies.append(
                remote(
                    buffer.at[y],
                    buffer.at[y],
                    (ring_send.at[phase, i], ring_recv.at[phase, i]),
                    peer,
                )
            )
        return copies

    def scatter(source, target, phase):
        copies = []
        for i, peer in enumerate(around):
            copies.append(
                remote(
                    source.at[peer[1] // 2],
                    target.at[y],
                    (ring_send.at[phase, i], ring_recv.at[phase, i]),
                    peer,
                )
            )
        return copies

    def arrive(copies):
        for copy in copies:
            copy.wait_recv()
        sent.extend(copies)

    def gathered(buffer):
        return jnp.concatenate(
            [buffer[i].astype(F32) for i in range(CHIPS)], axis=0
        ).astype(BF16)

    def total(buffer):
        out_sum = buffer[0].astype(F32)
        for i in range(1, CHIPS):
            out_sum = out_sum + buffer[i].astype(F32)
        return out_sum

    normed = normalize(rows_in, vector(0), vector(1))
    normed_all[y] = jnp.concatenate([normed, mine[:, D:].astype(BF16)], axis=1)
    copies = spread(normed_all, 0)

    for copy in started[2:]:
        copy.wait()
    for copy in pushed[:7]:
        copy.wait_recv()
    arrive(copies)

    everything = gathered(normed_all)
    row, lane = iotas((GROUP, LANES))
    key = everything[:, D:].astype(F32).astype(jnp.int32) + 4 * (row % 4)
    marks = one_hot(lane == key)
    same = matmul_t(marks, marks) > 0.5
    width = 6 * LANES
    qkv_bias = jnp.concatenate(
        [vec[core, 6:7, :width].astype(F32) for core in range(2)], axis=1
    )
    qkv = matmul_t(everything[:, :D], wqkv[...].reshape(2 * width, D)) + qkv_bias
    qkv = qkv.astype(BF16)
    scale = 1.0 / (float(HEAD_DIM) ** 0.5)
    attended = []
    for core in range(2):
        for head in range(2):
            base = core * width + head * LANES
            query = qkv[:, base : base + LANES]
            keys = qkv[:, base + 2 * LANES : base + 3 * LANES]
            values = qkv[:, base + 4 * LANES : base + 5 * LANES]
            scores = matmul_t(query, keys) * scale
            weights = jnp.where(same, jnp.exp(scores), 0.0)
            weights = weights / jnp.sum(weights, axis=1, keepdims=True)
            attended.append(matmul(weights.astype(BF16), values).astype(BF16))
    attended = jnp.concatenate(attended, axis=1)
    for copy in pushed[7:9]:
        copy.wait_recv()
    mixed_part = matmul(attended, wproj[...].reshape(4 * LANES, D))
    part_out[...] = mixed_part.reshape(CHIPS, ROWS, D).astype(BF16)
    part_in[y] = part_out[y]
    arrive(scatter(part_out, part_in, 1))

    mixed = (total(part_in) + vector(2) + rows_in).astype(BF16).astype(F32)
    normed2_all[y] = normalize(mixed, vector(3), vector(4))
    copies = spread(normed2_all, 2)
    for copy in pushed[9:]:
        copy.wait_recv()
    arrive(copies)

    fc1_bias = jnp.concatenate([vec[core, 7:8, :320].astype(F32) for core in range(2)], axis=1)
    lifted = matmul_t(gathered(normed2_all), wfc1[...].reshape(640, D)) + fc1_bias
    hidden = (lifted * jax.nn.sigmoid(1.702 * lifted)).astype(BF16)
    ffn_part = matmul(hidden, wfc2[...].reshape(640, D))
    ffn_out[...] = ffn_part.reshape(CHIPS, ROWS, D).astype(BF16)
    ffn_in[y] = ffn_out[y]
    arrive(scatter(ffn_out, ffn_in, 3))

    row, col = iotas((ROWS, D))
    slot = 4 * (2 * side + c) + row % 4
    encoded = jnp.where(slot < pair_count, total(ffn_in) + vector(5) + mixed, 0.0).astype(BF16)
    row, col = iotas((32, ROWS))
    inner = row % QUARTER
    pick = one_hot((inner < 12) & (col == (row // QUARTER) * 12 + inner))
    done_out[...] = matmul(pick, encoded).astype(BF16).reshape(2, QUARTER, D)
    done_in[0, c] = done_out[c]
    backs = []
    for i, (peer, block, where) in enumerate(
        ((beside[1], c, 1), (beside[2], 1 - c, 1), (beside[0], 1 - c, 0))
    ):
        backs.append(
            remote(
                done_out.at[block],
                done_in.at[where, c],
                (back_send.at[i], back_recv.at[i]),
                peer,
            )
        )
    arrive(backs)

    row, col = iotas((48, 64))
    inner = col % QUARTER
    pick = one_hot(
        (inner < 12)
        & (row == (inner // 4) * 16 + (col // QUARTER) * 4 + inner % 4)
        & (side == 0)
    )
    out[...] = matmul(pick, done_in[...].reshape(64, D)).astype(BF16).reshape(3, 16, D)
    for copy in sent:
        copy.wait_send()


def on_device(
    tiles,
    window_ids,
    counts,
    ln_gain,
    ln_bias,
    qkv_weight,
    qkv_bias,
    proj_weight,
    proj_bias,
    mlp_gain,
    mlp_bias,
    fc1_weight,
    fc1_bias,
    fc2_weight,
    fc2_bias,
):
    heads_bias = jnp.pad(qkv_bias.reshape(6, HEAD_DIM), ((0, 0), (0, LANES - HEAD_DIM)))
    vectors = jnp.stack(
        [
            ln_gain,
            ln_bias,
            proj_bias,
            mlp_gain,
            mlp_bias,
            fc2_bias,
            jnp.pad(heads_bias.reshape(768), (0, D - 768)),
            jnp.pad(fc1_bias, (0, D - 320)),
        ]
        + [jnp.zeros((D,), BF16)] * 8
    )
    vmem = pl.BlockSpec(memory_space=pltpu.VMEM)
    hbm = pl.BlockSpec(memory_space=pltpu.HBM)
    encoded = pl.pallas_call(
        encode,
        out_shape=jax.ShapeDtypeStruct((3, 16, D), BF16),
        in_specs=[pl.BlockSpec(memory_space=pltpu.SMEM), vmem, hbm, hbm, hbm, hbm, hbm, hbm],
        out_specs=vmem,
        scratch_shapes=[
            pltpu.VMEM((2, 16, D), BF16),
            pltpu.VMEM((2, 3, 2, LANES, D), BF16),
            pltpu.VMEM((2, 2, LANES, D), BF16),
            pltpu.VMEM((2, 320, D), BF16),
            pltpu.VMEM((2, 320, D), BF16),
            pltpu.VMEM((3, 16, D), BF16),
            pltpu.VMEM((4, QUARTER, WIDE), BF16),
            pltpu.VMEM((2, 2, QUARTER, WIDE), BF16),
            pltpu.VMEM((CHIPS, ROWS, WIDE), BF16),
            pltpu.VMEM((CHIPS, ROWS, D), BF16),
            pltpu.VMEM((CHIPS, ROWS, D), BF16),
            pltpu.VMEM((CHIPS, ROWS, D), BF16),
            pltpu.VMEM((CHIPS, ROWS, D), BF16),
            pltpu.VMEM((CHIPS, ROWS, D), BF16),
            pltpu.VMEM((2, QUARTER, D), BF16),
            pltpu.VMEM((2, 2, QUARTER, D), BF16),
            pltpu.SemaphoreType.DMA((12,)),
            pltpu.SemaphoreType.DMA((11,)),
            pltpu.SemaphoreType.DMA((11,)),
            pltpu.SemaphoreType.DMA((3,)),
            pltpu.SemaphoreType.DMA((3,)),
            pltpu.SemaphoreType.DMA((4, 3)),
            pltpu.SemaphoreType.DMA((4, 3)),
            pltpu.SemaphoreType.DMA((3,)),
            pltpu.SemaphoreType.DMA((3,)),
        ],
        compiler_params=pltpu.CompilerParams(
            collective_id=0, has_side_effects=True, vmem_limit_bytes=48 * 2**20
        ),
        name="encode",
    )(
        counts,
        jnp.transpose(window_ids),
        vectors,
        jnp.transpose(tiles, (1, 0, 2)),
        jnp.swapaxes(qkv_weight, 1, 2),
        proj_weight,
        jnp.transpose(fc1_weight),
        fc2_weight,
    )
    return jnp.transpose(encoded, (1, 0, 2))


def solution(mesh):
    placed = (
        P("dp", "tensor", None),
        P("dp", "tensor"),
        P(),
        P(),
        P(),
        P(None, None, "tensor"),
        P(None, "tensor"),
        P("tensor", None),
        P(),
        P(),
        P(),
        P(None, "tensor"),
        P("tensor"),
        P("tensor", None),
        P(),
    )
    return jax.shard_map(
        on_device, mesh=mesh, in_specs=placed, out_specs=P("dp", "tensor", None), check_vma=False
    )
```

```python
import jax
import jax.numpy as jnp
from jax import lax
from jax.experimental import pallas as pl
from jax.experimental.pallas import tpu as pltpu
from jax.sharding import PartitionSpec as P

D = 1280
HEAD_DIM = 80
LANES = 128
WIDE = D + LANES
QUARTER = 16
ROWS = 24
CHIPS = 4
GROUP = CHIPS * ROWS
MESH = pl.DeviceIdType.MESH
F32 = jnp.float32
BF16 = jnp.bfloat16


def matmul(left, right):
    return jnp.dot(left, right, preferred_element_type=F32)


def matmul_t(left, right):
    return lax.dot_general(left, right, (((1,), (1,)), ((), ())), preferred_element_type=F32)


def normalize(rows, gain, shift):
    centred = rows - jnp.mean(rows, axis=-1, keepdims=True)
    variance = jnp.mean(centred * centred, axis=-1, keepdims=True)
    return (centred * lax.rsqrt(variance + 1e-06) * gain + shift).astype(BF16)


def iotas(shape):
    return (
        lax.broadcasted_iota(jnp.int32, shape, 0),
        lax.broadcasted_iota(jnp.int32, shape, 1),
    )


def one_hot(flags):
    return jnp.where(flags, 1.0, 0.0).astype(BF16)


def encode(
    counts,
    window,
    tiles,
    ln_gain,
    ln_bias,
    qkv_weight,
    qkv_bias,
    proj_weight,
    proj_bias,
    mlp_gain,
    mlp_bias,
    fc1_weight,
    fc1_bias,
    fc2_weight,
    fc2_bias,
    out,
    count_all,
    window_rows,
    shifts,
    bias_qkv,
    fc1_own,
    fc1_other,
    vec,
    wqkv,
    wproj,
    wfc1,
    wfc2,
    tile_rows,
    quarter_out,
    quarter_in,
    normed_all,
    part_out,
    part_in,
    normed2_all,
    ffn_out,
    ffn_in,
    done_out,
    done_in,
    wide_bias,
    wide_fc1,
    early_sem,
    plain_sem,
    load_sem,
    weight_send,
    weight_recv,
    lend_send,
    lend_recv,
    ring_send,
    ring_recv,
    back_send,
    back_recv,
):
    d, t = lax.axis_index("dp"), lax.axis_index("tensor")
    y, c = t // 2, t % 2
    pd = (d + 32) % 64
    sib = y * 2 + (1 - c)
    around = [(d, ((y + k) % CHIPS) * 2 + c) for k in (2, 1, 3)]
    beside = [(d, sib), (pd, t), (pd, sib)]

    barrier = pltpu.get_barrier_semaphore()
    for peer in beside + around:
        pl.semaphore_signal(barrier, inc=1, device_id=peer, device_id_type=MESH)

    early = []
    for i, (src, dst) in enumerate(
        ((tiles, tile_rows), (window, window_rows), (counts, count_all))
    ):
        early.append(pltpu.make_async_copy(src, dst, early_sem.at[i]))
        early[-1].start()

    row, col = iotas((64, 48))
    inner = row % QUARTER
    pick = one_hot((inner < 12) & (col == (inner // 4) * 16 + (row // QUARTER) * 4 + inner % 4))
    early[0].wait()
    early[1].wait()
    row, col = iotas((16, 16))
    labels = []
    for token in range(3):
        picked = jnp.where(row == col, window_rows[token : token + 1, :].astype(F32), 0.0)
        labels.append(jnp.sum(picked, axis=1, keepdims=True))
    labels = jnp.broadcast_to(jnp.concatenate(labels, axis=0), (48, LANES)).astype(BF16)
    features = tile_rows[...].reshape(48, D)
    quarters = matmul(pick, jnp.concatenate([features, labels], axis=1))
    quarter_out[...] = quarters.astype(BF16).reshape(4, QUARTER, WIDE)
    quarter_in[0, c] = quarter_out[c]

    pl.semaphore_wait(barrier, len(beside) + len(around))

    def remote(src, dst, sems, peer):
        copy = pltpu.make_async_remote_copy(
            src_ref=src,
            dst_ref=dst,
            send_sem=sems[0],
            recv_sem=sems[1],
            device_id=peer,
            device_id_type=MESH,
        )
        copy.start()
        return copy

    sent = []
    lends = []
    for i, (peer, block, where) in enumerate(
        (
            (beside[1], 2 + c, 1),
            (beside[2], 3 - c, 1),
            (beside[0], 1 - c, 0),
        )
    ):
        lends.append(
            remote(
                quarter_out.at[block],
                quarter_in.at[where, c],
                (lend_send.at[i], lend_recv.at[i]),
                peer,
            )
        )

    pairs = [(qkv_bias, bias_qkv.at[c]), (fc1_bias, None)]
    for which in range(3):
        for head in range(2):
            pairs.append(
                (
                    qkv_weight.at[which, pl.ds(head * HEAD_DIM, HEAD_DIM)],
                    wqkv.at[c, which, head, pl.ds(0, HEAD_DIM)],
                )
            )
    for head in range(2):
        pairs.append(
            (
                proj_weight.at[pl.ds(head * HEAD_DIM, HEAD_DIM)],
                wproj.at[c, head, pl.ds(0, HEAD_DIM)],
            )
        )
    pairs += [(fc1_weight, wfc1.at[c]), (fc2_weight, wfc2.at[c])]
    pushed, loaded = [], []
    for i, (src, dst) in enumerate(pairs):
        there, here = (fc1_other, fc1_own) if dst is None else (dst, dst)
        pushed.append(remote(src, there, (weight_send.at[i], weight_recv.at[i]), beside[0]))
        loaded.append(pltpu.make_async_copy(src, here, load_sem.at[i]))
        loaded[-1].start()
    sent += lends + pushed
    plain = []
    for i, src in enumerate((ln_gain, ln_bias, proj_bias, mlp_gain, mlp_bias, fc2_bias)):
        plain.append(pltpu.make_async_copy(src, shifts[i], plain_sem.at[i]))
        plain[-1].start()

    gap = jnp.zeros((LANES - HEAD_DIM, D), BF16)
    for core in range(2):
        for head in range(2):
            for which in range(3):
                wqkv[core, which, head, HEAD_DIM:] = gap
            wproj[core, head, HEAD_DIM:] = gap
    early[2].wait()
    own_count = count_all[d]
    pair_count = own_count + count_all[pd]
    side = jnp.where(own_count > 0, 0, 1)
    for i, copy in enumerate(plain):
        copy.wait()
        vec[i : i + 1, :] = shifts[i][...].astype(F32).reshape(1, D)
    for copy in lends:
        copy.wait_recv()

    row, col = iotas((ROWS, 64))
    inner = col % QUARTER
    pick = one_hot(
        (inner < 12) & (col // 32 == side) & (row == ((col % 32) // QUARTER) * 12 + inner)
    )
    mine = matmul(pick, quarter_in[...].reshape(64, WIDE))
    rows_in = mine[:, :D]

    def vector(i):
        return vec[i : i + 1, :]

    def spread(buffer, phase):
        copies = []
        for i, peer in enumerate(around):
            copies.append(
                remote(
                    buffer.at[y],
                    buffer.at[y],
                    (ring_send.at[phase, i], ring_recv.at[phase, i]),
                    peer,
                )
            )
        return copies

    def scatter(source, target, phase):
        copies = []
        for i, peer in enumerate(around):
            copies.append(
                remote(
                    source.at[peer[1] // 2],
                    target.at[y],
                    (ring_send.at[phase, i], ring_recv.at[phase, i]),
                    peer,
                )
            )
        return copies

    def arrive(copies):
        for copy in copies:
            copy.wait_recv()
        sent.extend(copies)

    def gathered(buffer):
        return jnp.concatenate(
            [buffer[i].astype(F32) for i in range(CHIPS)], axis=0
        ).astype(BF16)

    def total(buffer):
        out_sum = buffer[0].astype(F32)
        for i in range(1, CHIPS):
            out_sum = out_sum + buffer[i].astype(F32)
        return out_sum

    normed = normalize(rows_in, vector(0), vector(1))
    normed_all[y] = jnp.concatenate([normed, mine[:, D:].astype(BF16)], axis=1)
    copies = spread(normed_all, 0)

    for copy in loaded:
        copy.wait()
    for copy in pushed[:2]:
        copy.wait_recv()
    zero = jnp.zeros((1, LANES - HEAD_DIM), F32)
    pieces = []
    for core in range(2):
        for which in range(3):
            bias = bias_qkv[core, which : which + 1, :].astype(F32)
            pieces += [bias[:, :HEAD_DIM], zero, bias[:, HEAD_DIM:], zero]
    wide_bias[...] = jnp.concatenate(pieces, axis=1)
    for copy in pushed[2:8]:
        copy.wait_recv()
    arrive(copies)

    everything = gathered(normed_all)
    row, lane = iotas((GROUP, LANES))
    key = everything[:, D:].astype(F32).astype(jnp.int32) + 4 * (row % 4)
    marks = one_hot(lane == key)
    same = matmul_t(marks, marks) > 0.5
    width = 6 * LANES
    qkv = matmul_t(everything[:, :D], wqkv[...].reshape(2 * width, D)) + wide_bias[...]
    qkv = qkv.astype(BF16)
    scale = 1.0 / (float(HEAD_DIM) ** 0.5)
    attended = []
    for core in range(2):
        for head in range(2):
            base = core * width + head * LANES
            query = qkv[:, base : base + LANES]
            keys = qkv[:, base + 2 * LANES : base + 3 * LANES]
            values = qkv[:, base + 4 * LANES : base + 5 * LANES]
            scores = matmul_t(query, keys) * scale
            weights = jnp.where(same, jnp.exp(scores), 0.0)
            weights = weights / jnp.sum(weights, axis=1, keepdims=True)
            attended.append(matmul(weights.astype(BF16), values).astype(BF16))
    attended = jnp.concatenate(attended, axis=1)
    for copy in pushed[8:10]:
        copy.wait_recv()
    mixed_part = matmul(attended, wproj[...].reshape(4 * LANES, D))
    part_out[...] = mixed_part.reshape(CHIPS, ROWS, D).astype(BF16)
    part_in[y] = part_out[y]
    arrive(scatter(part_out, part_in, 1))

    mixed = (total(part_in) + vector(2) + rows_in).astype(BF16).astype(F32)
    normed2_all[y] = normalize(mixed, vector(3), vector(4))
    copies = spread(normed2_all, 2)
    for copy in pushed[10:]:
        copy.wait_recv()
    own_bias = fc1_own[...].astype(F32).reshape(1, 320)
    other_bias = fc1_other[...].astype(F32).reshape(1, 320)
    wide_fc1[...] = jnp.concatenate(
        [jnp.where(c == 0, own_bias, other_bias), jnp.where(c == 0, other_bias, own_bias)], axis=1
    )
    arrive(copies)

    lifted = matmul_t(gathered(normed2_all), wfc1[...].reshape(640, D)) + wide_fc1[...]
    hidden = (lifted * jax.nn.sigmoid(1.702 * lifted)).astype(BF16)
    ffn_part = matmul(hidden, wfc2[...].reshape(640, D))
    ffn_out[...] = ffn_part.reshape(CHIPS, ROWS, D).astype(BF16)
    ffn_in[y] = ffn_out[y]
    arrive(scatter(ffn_out, ffn_in, 3))

    row, col = iotas((ROWS, D))
    slot = 4 * (2 * side + c) + row % 4
    encoded = jnp.where(slot < pair_count, total(ffn_in) + vector(5) + mixed, 0.0).astype(BF16)
    row, col = iotas((32, ROWS))
    inner = row % QUARTER
    pick = one_hot((inner < 12) & (col == (row // QUARTER) * 12 + inner))
    done_out[...] = matmul(pick, encoded).astype(BF16).reshape(2, QUARTER, D)
    done_in[0, c] = done_out[c]
    backs = []
    for i, (peer, block, where) in enumerate(
        ((beside[1], c, 1), (beside[2], 1 - c, 1), (beside[0], 1 - c, 0))
    ):
        backs.append(
            remote(
                done_out.at[block],
                done_in.at[where, c],
                (back_send.at[i], back_recv.at[i]),
                peer,
            )
        )
    arrive(backs)

    row, col = iotas((48, 64))
    inner = col % QUARTER
    pick = one_hot(
        (inner < 12)
        & (row == (inner // 4) * 16 + (col // QUARTER) * 4 + inner % 4)
        & (side == 0)
    )
    out[...] = matmul(pick, done_in[...].reshape(64, D)).astype(BF16).reshape(3, 16, D)
    for copy in sent:
        copy.wait_send()


def on_device(
    tiles,
    window_ids,
    counts,
    ln_gain,
    ln_bias,
    qkv_weight,
    qkv_bias,
    proj_weight,
    proj_bias,
    mlp_gain,
    mlp_bias,
    fc1_weight,
    fc1_bias,
    fc2_weight,
    fc2_bias,
):
    vmem = pl.BlockSpec(memory_space=pltpu.VMEM)
    hbm = pl.BlockSpec(memory_space=pltpu.HBM)
    encoded = pl.pallas_call(
        encode,
        out_shape=jax.ShapeDtypeStruct((3, 16, D), BF16),
        in_specs=[hbm] * 15,
        out_specs=vmem,
        scratch_shapes=[
            pltpu.SMEM((64,), jnp.int32),
            pltpu.VMEM((3, 16), jnp.int32),
            [pltpu.VMEM((D,), BF16)] * 6,
            pltpu.VMEM((2, 3, 160), BF16),
            pltpu.VMEM((320,), BF16),
            pltpu.VMEM((320,), BF16),
            pltpu.VMEM((8, D), F32),
            pltpu.VMEM((2, 3, 2, LANES, D), BF16),
            pltpu.VMEM((2, 2, LANES, D), BF16),
            pltpu.VMEM((2, 320, D), BF16),
            pltpu.VMEM((2, 320, D), BF16),
            pltpu.VMEM((3, 16, D), BF16),
            pltpu.VMEM((4, QUARTER, WIDE), BF16),
            pltpu.VMEM((2, 2, QUARTER, WIDE), BF16),
            pltpu.VMEM((CHIPS, ROWS, WIDE), BF16),
            pltpu.VMEM((CHIPS, ROWS, D), BF16),
            pltpu.VMEM((CHIPS, ROWS, D), BF16),
            pltpu.VMEM((CHIPS, ROWS, D), BF16),
            pltpu.VMEM((CHIPS, ROWS, D), BF16),
            pltpu.VMEM((CHIPS, ROWS, D), BF16),
            pltpu.VMEM((2, QUARTER, D), BF16),
            pltpu.VMEM((2, 2, QUARTER, D), BF16),
            pltpu.VMEM((1, 12 * LANES), F32),
            pltpu.VMEM((1, 640), F32),
            pltpu.SemaphoreType.DMA((3,)),
            pltpu.SemaphoreType.DMA((6,)),
            pltpu.SemaphoreType.DMA((12,)),
            pltpu.SemaphoreType.DMA((12,)),
            pltpu.SemaphoreType.DMA((12,)),
            pltpu.SemaphoreType.DMA((3,)),
            pltpu.SemaphoreType.DMA((3,)),
            pltpu.SemaphoreType.DMA((4, 3)),
            pltpu.SemaphoreType.DMA((4, 3)),
            pltpu.SemaphoreType.DMA((3,)),
            pltpu.SemaphoreType.DMA((3,)),
        ],
        compiler_params=pltpu.CompilerParams(
            collective_id=0, has_side_effects=True, vmem_limit_bytes=64 * 2**20
        ),
        name="encode",
    )(
        counts,
        jnp.transpose(window_ids),
        jnp.transpose(tiles, (1, 0, 2)),
        ln_gain,
        ln_bias,
        jnp.swapaxes(qkv_weight, 1, 2),
        qkv_bias,
        proj_weight,
        proj_bias,
        mlp_gain,
        mlp_bias,
        jnp.transpose(fc1_weight),
        fc1_bias,
        fc2_weight,
        fc2_bias,
    )
    return jnp.transpose(encoded, (1, 0, 2))


def solution(mesh):
    placed = (
        P("dp", "tensor", None),
        P("dp", "tensor"),
        P(),
        P(),
        P(),
        P(None, None, "tensor"),
        P(None, "tensor"),
        P("tensor", None),
        P(),
        P(),
        P(),
        P(None, "tensor"),
        P("tensor"),
        P("tensor", None),
        P(),
    )
    return jax.shard_map(
        on_device, mesh=mesh, in_specs=placed, out_specs=P("dp", "tensor", None), check_vma=False
    )
```

```python
import jax
import jax.numpy as jnp
from jax import lax
from jax.experimental import pallas as pl
from jax.experimental.pallas import tpu as pltpu
from jax.sharding import PartitionSpec as P

D = 1280
HEAD_DIM = 80
LANES = 128
WIDE = D + LANES
QUARTER = 16
ROWS = 24
CHIPS = 4
GROUP = CHIPS * ROWS
CHUNKS = 2
MESH = pl.DeviceIdType.MESH
F32 = jnp.float32
BF16 = jnp.bfloat16


def matmul(left, right):
    return jnp.dot(left, right, preferred_element_type=F32)


def matmul_t(left, right):
    return lax.dot_general(left, right, (((1,), (1,)), ((), ())), preferred_element_type=F32)


def normalize(rows, gain, shift):
    centred = rows - jnp.mean(rows, axis=-1, keepdims=True)
    variance = jnp.mean(centred * centred, axis=-1, keepdims=True)
    return (centred * lax.rsqrt(variance + 1e-06) * gain + shift).astype(BF16)


def iotas(shape):
    return (
        lax.broadcasted_iota(jnp.int32, shape, 0),
        lax.broadcasted_iota(jnp.int32, shape, 1),
    )


def one_hot(flags):
    return jnp.where(flags, 1.0, 0.0).astype(BF16)


def encode(
    counts,
    window,
    tiles,
    ln_gain,
    ln_bias,
    qkv_weight,
    qkv_bias,
    proj_weight,
    proj_bias,
    mlp_gain,
    mlp_bias,
    fc1_weight,
    fc1_bias,
    fc2_weight,
    fc2_bias,
    out,
    count_all,
    window_rows,
    shifts,
    bias_qkv,
    fc1_own,
    fc1_other,
    vec,
    wide_bias,
    wide_fc1,
    wqkv,
    wproj,
    wfc1,
    wfc2,
    tile_rows,
    quarter_out,
    quarter_in,
    kept,
    normed_all,
    part_out,
    part_in,
    normed2_all,
    ffn_out,
    ffn_in,
    done_out,
    done_in,
    early_sem,
    plain_sem,
    load_sem,
    weight_send,
    weight_recv,
    swap_send,
    swap_recv,
    ring_send,
    ring_recv,
    back_send,
    back_recv,
):
    d, t = lax.axis_index("dp"), lax.axis_index("tensor")
    y, c = t // 2, t % 2
    other = 1 - c
    beside = (d, y * 2 + other)
    around = [(d, ((y + k) % CHIPS) * 2 + c) for k in (2, 1, 3)]

    barrier = pltpu.get_barrier_semaphore()
    for peer in around + [beside]:
        pl.semaphore_signal(barrier, inc=1, device_id=peer, device_id_type=MESH)

    early = []
    for i, (src, dst) in enumerate(
        ((tiles, tile_rows), (window, window_rows), (counts, count_all))
    ):
        early.append(pltpu.make_async_copy(src, dst, early_sem.at[i]))
        early[-1].start()

    row, col = iotas((64, 48))
    inner = row % QUARTER
    pick = one_hot((inner < 12) & (col == (inner // 4) * 16 + (row // QUARTER) * 4 + inner % 4))
    early[1].wait()
    row, col = iotas((16, 16))
    labels = []
    for token in range(3):
        picked = jnp.where(row == col, window_rows[token : token + 1, :].astype(F32), 0.0)
        labels.append(jnp.sum(picked, axis=1, keepdims=True))
    labels = jnp.broadcast_to(jnp.concatenate(labels, axis=0), (48, LANES)).astype(BF16)
    early[0].wait()
    features = tile_rows[...].reshape(48, D)
    quarters = matmul(pick, jnp.concatenate([features, labels], axis=1))
    quarter_out[...] = quarters.astype(BF16).reshape(4, QUARTER, WIDE)

    pl.semaphore_wait(barrier, len(around) + 1)

    def remote(src, dst, send, recv, peer):
        copy = pltpu.make_async_remote_copy(
            src_ref=src,
            dst_ref=dst,
            send_sem=send,
            recv_sem=recv,
            device_id=peer,
            device_id_type=MESH,
        )
        copy.start()
        return copy

    sent = []
    swaps = []
    for k in range(CHUNKS):
        swaps.append(
            remote(
                quarter_out.at[2 * other + k],
                quarter_in.at[c, k],
                swap_send.at[k],
                swap_recv.at[k],
                beside,
            )
        )
    pairs = [(qkv_bias, bias_qkv.at[c]), (fc1_bias, None)]
    for which in range(3):
        for head in range(2):
            pairs.append(
                (
                    qkv_weight.at[which, pl.ds(head * HEAD_DIM, HEAD_DIM)],
                    wqkv.at[c, which, head, pl.ds(0, HEAD_DIM)],
                )
            )
    for head in range(2):
        pairs.append(
            (
                proj_weight.at[pl.ds(head * HEAD_DIM, HEAD_DIM)],
                wproj.at[c, head, pl.ds(0, HEAD_DIM)],
            )
        )
    pairs += [(fc1_weight, wfc1.at[c]), (fc2_weight, wfc2.at[c])]
    pushed, loaded = [], []
    for i, (src, dst) in enumerate(pairs):
        there, here = (fc1_other, fc1_own) if dst is None else (dst, dst)
        pushed.append(remote(src, there, weight_send.at[i], weight_recv.at[i], beside))
        loaded.append(pltpu.make_async_copy(src, here, load_sem.at[i]))
        loaded[-1].start()
    sent += swaps + pushed
    plain = []
    for i, src in enumerate((ln_gain, ln_bias, proj_bias, mlp_gain, mlp_bias, fc2_bias)):
        plain.append(pltpu.make_async_copy(src, shifts[i], plain_sem.at[i]))
        plain[-1].start()

    def vector(i):
        return vec[i : i + 1, :]

    def lay_out(i):
        plain[i].wait()
        vec[i : i + 1, :] = shifts[i][...].astype(F32).reshape(1, D)

    for k in range(CHUNKS):
        quarter_in[c, k] = quarter_out[2 * c + k]
    lay_out(0)
    lay_out(1)

    def spread(buffer, phase, k):
        copies = []
        for i, peer in enumerate(around):
            copies.append(
                remote(
                    buffer.at[k, y],
                    buffer.at[k, y],
                    ring_send.at[phase, k, i],
                    ring_recv.at[phase, k, i],
                    peer,
                )
            )
        return copies

    def scatter(source, target, phase, k):
        copies = []
        for i, peer in enumerate(around):
            copies.append(
                remote(
                    source.at[k, peer[1] // 2],
                    target.at[k, y],
                    ring_send.at[phase, k, i],
                    ring_recv.at[phase, k, i],
                    peer,
                )
            )
        target[k, y] = source[k, y]
        return copies

    def arrive(copies):
        for copy in copies:
            copy.wait_recv()
        sent.extend(copies)

    def gathered(buffer, k):
        return jnp.concatenate(
            [buffer[k, i].astype(F32) for i in range(CHIPS)], axis=0
        ).astype(BF16)

    def total(buffer, k):
        out_sum = buffer[k, 0].astype(F32)
        for i in range(1, CHIPS):
            out_sum = out_sum + buffer[k, i].astype(F32)
        return out_sum

    row, col = iotas((ROWS, 2 * QUARTER))
    inner = col % QUARTER
    pick = one_hot((inner < 12) & (row == (col // QUARTER) * 12 + inner))
    moving = []
    for k in range(CHUNKS):
        swaps[k].wait_recv()
        both = jnp.concatenate([quarter_in[0, k], quarter_in[1, k]], axis=0)
        mine = matmul(pick, both)
        kept[k] = mine[:, :D]
        normed = normalize(mine[:, :D], vector(0), vector(1))
        normed_all[k, y] = jnp.concatenate([normed, mine[:, D:].astype(BF16)], axis=1)
        moving.append(spread(normed_all, 0, k))

    for i in range(2, 6):
        lay_out(i)
    gap = jnp.zeros((LANES - HEAD_DIM, D), BF16)
    for core in range(2):
        for head in range(2):
            for which in range(3):
                wqkv[core, which, head, HEAD_DIM:] = gap
            wproj[core, head, HEAD_DIM:] = gap
    for copy in loaded:
        copy.wait()
    for copy in pushed[:2]:
        copy.wait_recv()
    zero = jnp.zeros((1, LANES - HEAD_DIM), F32)
    pieces = []
    for core in range(2):
        for which in range(3):
            bias = bias_qkv[core, which : which + 1, :].astype(F32)
            pieces += [bias[:, :HEAD_DIM], zero, bias[:, HEAD_DIM:], zero]
    wide_bias[...] = jnp.concatenate(pieces, axis=1)
    own_bias = fc1_own[...].astype(F32).reshape(1, 320)
    other_bias = fc1_other[...].astype(F32).reshape(1, 320)
    wide_fc1[...] = jnp.concatenate(
        [jnp.where(c == 0, own_bias, other_bias), jnp.where(c == 0, other_bias, own_bias)], axis=1
    )
    for copy in pushed[2:10]:
        copy.wait_recv()
    early[2].wait()
    own_count = count_all[d]

    width = 6 * LANES
    scale = 1.0 / (float(HEAD_DIM) ** 0.5)
    summing = []
    for k in range(CHUNKS):
        arrive(moving[k])
        everything = gathered(normed_all, k)
        row, lane = iotas((GROUP, LANES))
        key = everything[:, D:].astype(F32).astype(jnp.int32) + 4 * (row % 4)
        marks = one_hot(lane == key)
        same = matmul_t(marks, marks) > 0.5
        qkv = matmul_t(everything[:, :D], wqkv[...].reshape(2 * width, D)) + wide_bias[...]
        qkv = qkv.astype(BF16)
        attended = []
        for core in range(2):
            for head in range(2):
                base = core * width + head * LANES
                query = qkv[:, base : base + LANES]
                keys = qkv[:, base + 2 * LANES : base + 3 * LANES]
                values = qkv[:, base + 4 * LANES : base + 5 * LANES]
                scores = matmul_t(query, keys) * scale
                weights = jnp.where(same, jnp.exp(scores), 0.0)
                weights = weights / jnp.sum(weights, axis=1, keepdims=True)
                attended.append(matmul(weights.astype(BF16), values).astype(BF16))
        attended = jnp.concatenate(attended, axis=1)
        mixed_part = matmul(attended, wproj[...].reshape(4 * LANES, D))
        part_out[k] = mixed_part.reshape(CHIPS, ROWS, D).astype(BF16)
        summing.append(scatter(part_out, part_in, 1, k))

    moving = []
    for k in range(CHUNKS):
        arrive(summing[k])
        mixed = (total(part_in, k) + vector(2) + kept[k]).astype(BF16).astype(F32)
        kept[k] = mixed
        normed2_all[k, y] = normalize(mixed, vector(3), vector(4))
        moving.append(spread(normed2_all, 2, k))

    for copy in pushed[10:]:
        copy.wait_recv()
    summing = []
    for k in range(CHUNKS):
        arrive(moving[k])
        lifted = matmul_t(gathered(normed2_all, k), wfc1[...].reshape(640, D)) + wide_fc1[...]
        hidden = (lifted * jax.nn.sigmoid(1.702 * lifted)).astype(BF16)
        ffn_part = matmul(hidden, wfc2[...].reshape(640, D))
        ffn_out[k] = ffn_part.reshape(CHIPS, ROWS, D).astype(BF16)
        summing.append(scatter(ffn_out, ffn_in, 3, k))

    row, col = iotas((2 * QUARTER, ROWS))
    inner = row % QUARTER
    pick = one_hot((inner < 12) & (col == (row // QUARTER) * 12 + inner))
    row, col = iotas((ROWS, D))
    backs = []
    for k in range(CHUNKS):
        arrive(summing[k])
        slot = 8 * c + 4 * k + row % 4
        encoded = total(ffn_in, k) + vector(5) + kept[k]
        encoded = jnp.where(slot < own_count, encoded, 0.0).astype(BF16)
        done_out[k] = matmul(pick, encoded).astype(BF16).reshape(2, QUARTER, D)
        backs.append(
            remote(
                done_out.at[k, other],
                done_in.at[c, k],
                back_send.at[k],
                back_recv.at[k],
                beside,
            )
        )
        done_in[c, k] = done_out[k, c]
    arrive(backs)

    row, col = iotas((48, 64))
    inner = col % QUARTER
    pick = one_hot(
        (inner < 12) & (row == (inner // 4) * 16 + (col // QUARTER) * 4 + inner % 4)
    )
    out[...] = matmul(pick, done_in[...].reshape(64, D)).astype(BF16).reshape(3, 16, D)
    for copy in sent:
        copy.wait_send()


def on_device(
    tiles,
    window_ids,
    counts,
    ln_gain,
    ln_bias,
    qkv_weight,
    qkv_bias,
    proj_weight,
    proj_bias,
    mlp_gain,
    mlp_bias,
    fc1_weight,
    fc1_bias,
    fc2_weight,
    fc2_bias,
):
    operands = (
        counts,
        jnp.transpose(window_ids),
        jnp.transpose(tiles, (1, 0, 2)),
        ln_gain,
        ln_bias,
        jnp.swapaxes(qkv_weight, 1, 2),
        qkv_bias,
        proj_weight,
        proj_bias,
        mlp_gain,
        mlp_bias,
        jnp.transpose(fc1_weight),
        fc1_bias,
        fc2_weight,
        fc2_bias,
    )
    encoded = pl.pallas_call(
        encode,
        out_shape=pltpu.VMEM((3, 16, D), BF16),
        in_specs=[pl.BlockSpec(memory_space=pltpu.HBM)] * len(operands),
        out_specs=pl.BlockSpec(memory_space=pltpu.VMEM),
        scratch_shapes=[
            pltpu.SMEM((64,), jnp.int32),
            pltpu.VMEM((3, 16), jnp.int32),
            [pltpu.VMEM((D,), BF16)] * 6,
            pltpu.VMEM((2, 3, 160), BF16),
            pltpu.VMEM((320,), BF16),
            pltpu.VMEM((320,), BF16),
            pltpu.VMEM((8, D), F32),
            pltpu.VMEM((1, 12 * LANES), F32),
            pltpu.VMEM((1, 640), F32),
            pltpu.VMEM((2, 3, 2, LANES, D), BF16),
            pltpu.VMEM((2, 2, LANES, D), BF16),
            pltpu.VMEM((2, 320, D), BF16),
            pltpu.VMEM((2, 320, D), BF16),
            pltpu.VMEM((3, 16, D), BF16),
            pltpu.VMEM((4, QUARTER, WIDE), BF16),
            pltpu.VMEM((2, CHUNKS, QUARTER, WIDE), BF16),
            pltpu.VMEM((CHUNKS, ROWS, D), F32),
            pltpu.VMEM((CHUNKS, CHIPS, ROWS, WIDE), BF16),
            pltpu.VMEM((CHUNKS, CHIPS, ROWS, D), BF16),
            pltpu.VMEM((CHUNKS, CHIPS, ROWS, D), BF16),
            pltpu.VMEM((CHUNKS, CHIPS, ROWS, D), BF16),
            pltpu.VMEM((CHUNKS, CHIPS, ROWS, D), BF16),
            pltpu.VMEM((CHUNKS, CHIPS, ROWS, D), BF16),
            pltpu.VMEM((CHUNKS, 2, QUARTER, D), BF16),
            pltpu.VMEM((2, CHUNKS, QUARTER, D), BF16),
            pltpu.SemaphoreType.DMA((3,)),
            pltpu.SemaphoreType.DMA((6,)),
            pltpu.SemaphoreType.DMA((12,)),
            pltpu.SemaphoreType.DMA((12,)),
            pltpu.SemaphoreType.DMA((12,)),
            pltpu.SemaphoreType.DMA((CHUNKS,)),
            pltpu.SemaphoreType.DMA((CHUNKS,)),
            pltpu.SemaphoreType.DMA((4, CHUNKS, 3)),
            pltpu.SemaphoreType.DMA((4, CHUNKS, 3)),
            pltpu.SemaphoreType.DMA((CHUNKS,)),
            pltpu.SemaphoreType.DMA((CHUNKS,)),
        ],
        compiler_params=pltpu.CompilerParams(
            collective_id=0, has_side_effects=True, vmem_limit_bytes=48 * 2**20
        ),
        name="encode",
    )(*(pltpu.with_memory_space_constraint(operand, pltpu.HBM) for operand in operands))
    return jnp.transpose(encoded, (1, 0, 2))


def solution(mesh):
    placed = (
        P("dp", "tensor", None),
        P("dp", "tensor"),
        P(),
        P(),
        P(),
        P(None, None, "tensor"),
        P(None, "tensor"),
        P("tensor", None),
        P(),
        P(),
        P(),
        P(None, "tensor"),
        P("tensor"),
        P("tensor", None),
        P(),
    )
    return jax.shard_map(
        on_device, mesh=mesh, in_specs=placed, out_specs=P("dp", "tensor", None), check_vma=False
    )
```

```python
import jax
import jax.numpy as jnp
from jax import lax
from jax.experimental import pallas as pl
from jax.experimental.pallas import tpu as pltpu
from jax.sharding import PartitionSpec as P

D = 1280
HEAD_DIM = 80
LANES = 128
WIDE = D + LANES
QUARTER = 16
ROWS = 24
CHIPS = 4
GROUP = CHIPS * ROWS
CHUNKS = 2
HALF = 32
HEAD_LANES = 384
MESH = pl.DeviceIdType.MESH
F32 = jnp.float32
BF16 = jnp.bfloat16


def matmul(left, right):
    return jnp.dot(left, right, preferred_element_type=F32)


def matmul_t(left, right):
    return lax.dot_general(left, right, (((1,), (1,)), ((), ())), preferred_element_type=F32)


def normalize(rows, gain, shift):
    centred = rows - jnp.mean(rows, axis=-1, keepdims=True)
    variance = jnp.mean(centred * centred, axis=-1, keepdims=True)
    return (centred * lax.rsqrt(variance + 1e-06) * gain + shift).astype(BF16)


def iotas(shape):
    return (
        lax.broadcasted_iota(jnp.int32, shape, 0),
        lax.broadcasted_iota(jnp.int32, shape, 1),
    )


def one_hot(flags):
    return jnp.where(flags, 1.0, 0.0).astype(BF16)


def encode(
    counts,
    window,
    tiles,
    ln_gain,
    ln_bias,
    qkv_weight,
    qkv_bias,
    proj_weight,
    proj_bias,
    mlp_gain,
    mlp_bias,
    fc1_weight,
    fc1_bias,
    fc2_weight,
    fc2_bias,
    out,
    count_all,
    window_rows,
    shifts,
    bias_qkv,
    fc1_own,
    fc1_other,
    vec,
    wide_bias,
    wide_fc1,
    wqkv,
    wproj,
    wfc1,
    wfc2,
    tile_rows,
    quarter_out,
    quarter_in,
    kept,
    lent_out,
    lent_in,
    normed_all,
    normed_lent,
    lent_block,
    part_out,
    part_in,
    normed2_all,
    ffn_out,
    ffn_in,
    done_out,
    done_in,
    early_sem,
    plain_sem,
    load_sem,
    weight_send,
    weight_recv,
    swap_send,
    swap_recv,
    lend_send,
    lend_recv,
    ring_send,
    ring_recv,
    back_send,
    back_recv,
):
    d, t = lax.axis_index("dp"), lax.axis_index("tensor")
    y, c = t // 2, t % 2
    other = 1 - c
    beside = (d, y * 2 + other)
    partner = (d + HALF) % (2 * HALF)
    around = [(d, ((y + k) % CHIPS) * 2 + c) for k in (2, 1, 3)]
    across = [(partner, ((y + k) % CHIPS) * 2 + c) for k in (2, 1, 3, 0)]

    barrier = pltpu.get_barrier_semaphore()
    for peer in around + across + [beside]:
        pl.semaphore_signal(barrier, inc=1, device_id=peer, device_id_type=MESH)

    early = []
    for i, (src, dst) in enumerate(
        ((tiles, tile_rows), (window, window_rows), (counts, count_all))
    ):
        early.append(pltpu.make_async_copy(src, dst, early_sem.at[i]))
        early[-1].start()

    row, col = iotas((64, 48))
    inner = row % QUARTER
    pick = one_hot((inner < 12) & (col == (inner // 4) * 16 + (row // QUARTER) * 4 + inner % 4))
    early[1].wait()
    row, col = iotas((16, 16))
    labels = []
    for token in range(3):
        picked = jnp.where(row == col, window_rows[token : token + 1, :].astype(F32), 0.0)
        labels.append(jnp.sum(picked, axis=1, keepdims=True))
    labels = jnp.broadcast_to(jnp.concatenate(labels, axis=0), (48, LANES)).astype(BF16)
    early[0].wait()
    features = tile_rows[...].reshape(48, D)
    quarters = matmul(pick, jnp.concatenate([features, labels], axis=1))
    quarter_out[...] = quarters.astype(BF16).reshape(4, QUARTER, WIDE)

    pl.semaphore_wait(barrier, len(around) + len(across) + 1)

    def remote(src, dst, send, recv, peer):
        copy = pltpu.make_async_remote_copy(
            src_ref=src,
            dst_ref=dst,
            send_sem=send,
            recv_sem=recv,
            device_id=peer,
            device_id_type=MESH,
        )
        copy.start()
        return copy

    sent = []
    swaps = []
    for k in range(CHUNKS):
        swaps.append(
            remote(
                quarter_out.at[other + 2 * k],
                quarter_in.at[c, k],
                swap_send.at[k],
                swap_recv.at[k],
                beside,
            )
        )
    sent += swaps
    plain = []
    for i, src in enumerate((ln_gain, ln_bias, proj_bias, mlp_gain, mlp_bias, fc2_bias)):
        plain.append(pltpu.make_async_copy(src, shifts[i], plain_sem.at[i]))
        plain[-1].start()

    def vector(i):
        return vec[i : i + 1, :]

    def lay_out(i):
        plain[i].wait()
        vec[i : i + 1, :] = shifts[i][...].astype(F32).reshape(1, D)

    for k in range(CHUNKS):
        quarter_in[c, k] = quarter_out[c + 2 * k]
    lay_out(0)
    lay_out(1)

    def spread(buffer, phase, lent=None, landing=None):
        copies = []
        for i in range(CHIPS):
            if lent is not None:
                copies.append(
                    remote(
                        lent,
                        landing.at[y],
                        lend_send.at[phase, i],
                        lend_recv.at[phase, i],
                        across[i],
                    )
                )
            if i < len(around):
                copies.append(
                    remote(
                        buffer.at[y],
                        buffer.at[y],
                        ring_send.at[phase, i],
                        ring_recv.at[phase, i],
                        around[i],
                    )
                )
        return copies

    def scatter(source, target, phase, landing=None):
        copies = []
        for i in range(CHIPS):
            if landing is not None:
                copies.append(
                    remote(
                        source.at[across[i][1] // 2],
                        landing.at[y],
                        lend_send.at[phase, i],
                        lend_recv.at[phase, i],
                        across[i],
                    )
                )
            if i < len(around):
                copies.append(
                    remote(
                        source.at[around[i][1] // 2],
                        target.at[y],
                        ring_send.at[phase, i],
                        ring_recv.at[phase, i],
                        around[i],
                    )
                )
        target[y] = source[y]
        return copies

    def arrive(copies):
        for copy in copies:
            copy.wait_recv()
        sent.extend(copies)

    def gathered(buffer):
        return jnp.concatenate([buffer[i].astype(F32) for i in range(CHIPS)], axis=0)

    def total(buffer):
        out_sum = buffer[0].astype(F32)
        for i in range(1, CHIPS):
            out_sum = out_sum + buffer[i].astype(F32)
        return out_sum

    row, col = iotas((ROWS, 2 * QUARTER))
    inner = col % QUARTER
    pick = one_hot((inner < 12) & (row == (col // QUARTER) * 12 + inner))
    for k in range(CHUNKS):
        swaps[k].wait_recv()
        both = jnp.concatenate([quarter_in[0, k], quarter_in[1, k]], axis=0)
        mine = matmul(pick, both)
        normed = normalize(mine[:, :D], vector(0), vector(1))
        block = jnp.concatenate([normed, mine[:, D:].astype(BF16)], axis=1)
        if k == 0:
            kept[...] = mine[:, :D]
            normed_all[y] = block
        else:
            lent_out[...] = mine[:, :D].astype(BF16)
            lent_block[...] = block
    moving = spread(normed_all, 0, lent_block, normed_lent)
    residual = remote(lent_out, lent_in, swap_send.at[CHUNKS], swap_recv.at[CHUNKS], across[3])

    mine_at = pl.multiple_of(c * 160, 16)
    pairs = [(qkv_bias, bias_qkv.at[c]), (fc1_bias, None)]
    for which, start in enumerate((0, HEAD_LANES, HEAD_LANES + 320)):
        pairs.append((qkv_weight.at[which], wqkv.at[pl.ds(start + mine_at, 160)]))
    pairs.append((proj_weight, wproj.at[pl.ds(64 + mine_at, 160)]))
    pairs += [(fc1_weight, wfc1.at[c]), (fc2_weight, wfc2.at[c])]
    pushed, loaded = [], []
    for i, (src, dst) in enumerate(pairs):
        there, here = (fc1_other, fc1_own) if dst is None else (dst, dst)
        pushed.append(remote(src, there, weight_send.at[i], weight_recv.at[i], beside))
        loaded.append(pltpu.make_async_copy(src, here, load_sem.at[i]))
        loaded[-1].start()
    sent += pushed
    for i in range(2, 6):
        lay_out(i)
    gap = jnp.zeros((64, D), BF16)
    wqkv[320:HEAD_LANES, :] = gap
    wproj[0:64, :] = gap
    for copy in loaded:
        copy.wait()
    for copy in pushed[:2]:
        copy.wait_recv()
    pieces = []
    for which in range(3):
        for core in range(2):
            pieces.append(bias_qkv[core, which : which + 1, :].astype(F32))
        if which == 0:
            pieces.append(jnp.zeros((1, 64), F32))
    wide_bias[...] = jnp.concatenate(pieces, axis=1)
    own_bias = fc1_own[...].astype(F32).reshape(1, 320)
    other_bias = fc1_other[...].astype(F32).reshape(1, 320)
    wide_fc1[...] = jnp.concatenate(
        [jnp.where(c == 0, own_bias, other_bias), jnp.where(c == 0, other_bias, own_bias)], axis=1
    )
    for copy in pushed[2:6]:
        copy.wait_recv()
    early[2].wait()
    own_count = count_all[d]
    owner = own_count > 0

    scale = 1.0 / (float(HEAD_DIM) ** 0.5)
    arrive(moving)
    everything = jnp.where(owner, gathered(normed_all), gathered(normed_lent))
    row, lane = iotas((GROUP, LANES))
    marks = one_hot(lane == everything[:, D:].astype(jnp.int32) + 4 * (row % 4))
    same = matmul_t(marks, marks) > 0.5
    qkv = matmul_t(everything[:, :D].astype(BF16), wqkv[...]) + wide_bias[...]
    qkv = qkv.astype(BF16)
    row, lane = iotas((GROUP, HEAD_LANES))
    query, keys, values = (
        qkv[:, start : start + HEAD_LANES] for start in (0, HEAD_LANES, 2 * HEAD_LANES - LANES)
    )
    heads = [(lane >= HEAD_DIM * j) & (lane < HEAD_DIM * (j + 1)) for j in range(4)]
    query = jnp.concatenate([jnp.where(mask, query, 0.0).astype(BF16) for mask in heads], axis=0)
    scores = matmul_t(query, keys) * scale
    same = jnp.concatenate([same] * 4, axis=0)
    weights = jnp.where(same, jnp.exp(scores), 0.0)
    weights = weights / jnp.sum(weights, axis=1, keepdims=True)
    mixture = matmul(weights.astype(BF16), values)
    attended = jnp.zeros((GROUP, HEAD_LANES), F32)
    for j in range(4):
        mask = (lane >= 64 + HEAD_DIM * j) & (lane < 64 + HEAD_DIM * (j + 1))
        attended = jnp.where(mask, mixture[GROUP * j : GROUP * (j + 1)], attended)
    mixed_part = matmul(attended.astype(BF16), wproj[...])
    part_out[...] = mixed_part.reshape(CHIPS, ROWS, D).astype(BF16)
    summing = scatter(part_out, part_in, 1)
    residual.wait_recv()
    sent.append(residual)
    carried = jnp.where(owner, kept[...], lent_in[...].astype(F32)) + vector(2)
    arrive(summing)

    mixed = (total(part_in) + carried).astype(BF16).astype(F32)
    kept[...] = mixed + vector(5)
    normed2_all[y] = normalize(mixed, vector(3), vector(4))
    moving = spread(normed2_all, 2)
    for copy in pushed[6:]:
        copy.wait_recv()
    arrive(moving)

    lifted = matmul_t(gathered(normed2_all).astype(BF16), wfc1[...].reshape(640, D)) + wide_fc1[...]
    hidden = (lifted * jax.nn.sigmoid(1.702 * lifted)).astype(BF16)
    ffn_part = matmul(hidden, wfc2[...].reshape(640, D))
    for i in range(CHIPS):
        block = ffn_part[ROWS * i : ROWS * (i + 1)] + jnp.where(y == i, kept[...], 0.0)
        ffn_out[i] = block.astype(BF16)
    summing = scatter(ffn_out, ffn_in.at[0], 3, ffn_in.at[1])

    row, col = iotas((2 * QUARTER, ROWS))
    inner = row % QUARTER
    pick = one_hot((inner < 12) & (col == (row // QUARTER) * 12 + inner))
    row, col = iotas((ROWS, D))
    arrive(summing)
    backs = []
    for k in range(CHUNKS):
        slot = 4 * c + 8 * k + row % 4
        encoded = jnp.where(slot < own_count, total(ffn_in.at[k]), 0.0).astype(BF16)
        done_out[k] = matmul(pick, encoded).astype(BF16).reshape(2, QUARTER, D)
        backs.append(
            remote(
                done_out.at[k, other],
                done_in.at[c, k],
                back_send.at[k],
                back_recv.at[k],
                beside,
            )
        )
        done_in[c, k] = done_out[k, c]
    arrive(backs)

    row, col = iotas((48, 64))
    inner = col % QUARTER
    pick = one_hot(
        (inner < 12)
        & (
            row
            == (inner // 4) * 16 + 4 * (col // (2 * QUARTER)) + 8 * (col // QUARTER % 2) + inner % 4
        )
    )
    out[...] = matmul(pick, done_in[...].reshape(64, D)).astype(BF16).reshape(3, 16, D)
    for copy in sent:
        copy.wait_send()


def on_device(
    tiles,
    window_ids,
    counts,
    ln_gain,
    ln_bias,
    qkv_weight,
    qkv_bias,
    proj_weight,
    proj_bias,
    mlp_gain,
    mlp_bias,
    fc1_weight,
    fc1_bias,
    fc2_weight,
    fc2_bias,
):
    operands = (
        counts,
        jnp.transpose(window_ids),
        jnp.transpose(tiles, (1, 0, 2)),
        ln_gain,
        ln_bias,
        jnp.swapaxes(qkv_weight, 1, 2),
        qkv_bias,
        proj_weight,
        proj_bias,
        mlp_gain,
        mlp_bias,
        jnp.transpose(fc1_weight),
        fc1_bias,
        fc2_weight,
        fc2_bias,
    )
    encoded = pl.pallas_call(
        encode,
        out_shape=pltpu.VMEM((3, 16, D), BF16),
        in_specs=[pl.BlockSpec(memory_space=pltpu.HBM)] * len(operands),
        out_specs=pl.BlockSpec(memory_space=pltpu.VMEM),
        scratch_shapes=[
            pltpu.SMEM((64,), jnp.int32),
            pltpu.VMEM((3, 16), jnp.int32),
            [pltpu.VMEM((D,), BF16)] * 6,
            pltpu.VMEM((2, 3, 160), BF16),
            pltpu.VMEM((320,), BF16),
            pltpu.VMEM((320,), BF16),
            pltpu.VMEM((8, D), F32),
            pltpu.VMEM((1, 1024), F32),
            pltpu.VMEM((1, 640), F32),
            pltpu.VMEM((1024, D), BF16),
            pltpu.VMEM((HEAD_LANES, D), BF16),
            pltpu.VMEM((2, 320, D), BF16),
            pltpu.VMEM((2, 320, D), BF16),
            pltpu.VMEM((3, 16, D), BF16),
            pltpu.VMEM((4, QUARTER, WIDE), BF16),
            pltpu.VMEM((2, CHUNKS, QUARTER, WIDE), BF16),
            pltpu.VMEM((ROWS, D), F32),
            pltpu.VMEM((ROWS, D), BF16),
            pltpu.VMEM((ROWS, D), BF16),
            pltpu.VMEM((CHIPS, ROWS, WIDE), BF16),
            pltpu.VMEM((CHIPS, ROWS, WIDE), BF16),
            pltpu.VMEM((ROWS, WIDE), BF16),
            pltpu.VMEM((CHIPS, ROWS, D), BF16),
            pltpu.VMEM((CHIPS, ROWS, D), BF16),
            pltpu.VMEM((CHIPS, ROWS, D), BF16),
            pltpu.VMEM((CHIPS, ROWS, D), BF16),
            pltpu.VMEM((CHUNKS, CHIPS, ROWS, D), BF16),
            pltpu.VMEM((CHUNKS, 2, QUARTER, D), BF16),
            pltpu.VMEM((2, CHUNKS, QUARTER, D), BF16),
            pltpu.SemaphoreType.DMA((3,)),
            pltpu.SemaphoreType.DMA((6,)),
            pltpu.SemaphoreType.DMA((8,)),
            pltpu.SemaphoreType.DMA((8,)),
            pltpu.SemaphoreType.DMA((8,)),
            pltpu.SemaphoreType.DMA((CHUNKS + 1,)),
            pltpu.SemaphoreType.DMA((CHUNKS + 1,)),
            pltpu.SemaphoreType.DMA((4, 4)),
            pltpu.SemaphoreType.DMA((4, 4)),
            pltpu.SemaphoreType.DMA((4, 3)),
            pltpu.SemaphoreType.DMA((4, 3)),
            pltpu.SemaphoreType.DMA((CHUNKS,)),
            pltpu.SemaphoreType.DMA((CHUNKS,)),
        ],
        compiler_params=pltpu.CompilerParams(
            collective_id=0, has_side_effects=True, vmem_limit_bytes=48 * 2**20
        ),
        name="encode",
    )(*(pltpu.with_memory_space_constraint(operand, pltpu.HBM) for operand in operands))
    return jnp.transpose(encoded, (1, 0, 2))


def solution(mesh):
    placed = (
        P("dp", "tensor", None),
        P("dp", "tensor"),
        P(),
        P(),
        P(),
        P(None, None, "tensor"),
        P(None, "tensor"),
        P("tensor", None),
        P(),
        P(),
        P(),
        P(None, "tensor"),
        P("tensor"),
        P("tensor", None),
        P(),
    )
    return jax.shard_map(
        on_device, mesh=mesh, in_specs=placed, out_specs=P("dp", "tensor", None), check_vma=False
    )
```

```python
import jax
import jax.numpy as jnp
from jax import lax
from jax.experimental import pallas as pl
from jax.experimental.pallas import tpu as pltpu
from jax.sharding import PartitionSpec as P

D = 1280
HEAD_DIM = 80
CHIPS = 4
SLOTS = 16
HALF = SLOTS // 2
TOKENS = 3
ROWS = TOKENS * HALF
GROUP = CHIPS * ROWS
HEADS = 4
HEAD_LANES = 384
MESH = pl.DeviceIdType.MESH
F32 = jnp.float32
BF16 = jnp.bfloat16


def matmul(left, right):
    return jnp.dot(left, right, preferred_element_type=F32)


def matmul_t(left, right):
    return lax.dot_general(left, right, (((1,), (1,)), ((), ())), preferred_element_type=F32)


def normalize(rows, gain, shift):
    centred = rows - jnp.mean(rows, axis=-1, keepdims=True)
    variance = jnp.mean(centred * centred, axis=-1, keepdims=True)
    return centred * lax.rsqrt(variance + 1e-06) * gain + shift


def iotas(shape):
    return (
        lax.broadcasted_iota(jnp.int32, shape, 0),
        lax.broadcasted_iota(jnp.int32, shape, 1),
    )


def one_hot(flags):
    return jnp.where(flags, 1.0, 0.0).astype(BF16)


def encode(
    counts,
    window,
    tiles,
    ln_gain,
    ln_bias,
    qkv_weight,
    qkv_bias,
    proj_weight,
    proj_bias,
    mlp_gain,
    mlp_bias,
    fc1_weight,
    fc1_bias,
    fc2_weight,
    fc2_bias,
    out,
    count_all,
    window_all,
    label_rows,
    shifts,
    bias_qkv,
    fc1_own,
    fc1_other,
    vec,
    wide_bias,
    wide_fc1,
    wqkv,
    wproj,
    wfc1,
    wfc2,
    tile_rows,
    swap_out,
    raw_out,
    raw_in,
    kept,
    normed_all,
    part_out,
    part_in,
    normed2_all,
    ffn_out,
    ffn_in,
    done_out,
    done_in,
    early_sem,
    plain_sem,
    load_sem,
    weight_send,
    weight_recv,
    label_send,
    label_recv,
    swap_send,
    swap_recv,
    ring_send,
    ring_recv,
):
    d, t = lax.axis_index("dp"), lax.axis_index("tensor")
    y, c = t // 2, t % 2
    other = 1 - c
    beside = (d, y * 2 + other)
    around = [(d, ((y + k) % CHIPS) * 2 + c) for k in (2, 1, 3)]

    barrier = pltpu.get_barrier_semaphore()
    for peer in around + [beside]:
        pl.semaphore_signal(barrier, inc=1, device_id=peer, device_id_type=MESH)

    early = []
    for i, (src, dst) in enumerate(
        ((tiles, tile_rows), (window, window_all.at[t]), (counts, count_all))
    ):
        early.append(pltpu.make_async_copy(src, dst, early_sem.at[i]))
        early[-1].start()
    plain = []
    for i, src in enumerate((ln_gain, ln_bias, proj_bias, mlp_gain, mlp_bias, fc2_bias)):
        plain.append(pltpu.make_async_copy(src, shifts[i], plain_sem.at[i]))
        plain[-1].start()

    def vector(i):
        return vec[i : i + 1, :]

    def lay_out(i):
        plain[i].wait()
        vec[i : i + 1, :] = shifts[i][...].astype(F32).reshape(1, D)

    def halves(rows):
        low = [rows[SLOTS * i : SLOTS * i + HALF] for i in range(TOKENS)]
        high = [rows[SLOTS * i + HALF : SLOTS * (i + 1)] for i in range(TOKENS)]
        low, high = jnp.concatenate(low, axis=0), jnp.concatenate(high, axis=0)
        return jnp.where(c == 0, low, high), jnp.where(c == 0, high, low)

    lay_out(0)
    lay_out(1)
    early[0].wait()
    features = tile_rows[...].astype(F32).reshape(TOKENS * SLOTS, D)
    mine, theirs = halves(normalize(features, vector(0), vector(1)))
    swap_out[...] = theirs.astype(BF16)
    normed_all[1, y] = mine.astype(BF16)

    pl.semaphore_wait(barrier, len(around) + 1)

    def remote(src, dst, send, recv, peer):
        copy = pltpu.make_async_remote_copy(
            src_ref=src,
            dst_ref=dst,
            send_sem=send,
            recv_sem=recv,
            device_id=peer,
            device_id_type=MESH,
        )
        copy.start()
        return copy

    def spread(buffer, phase, k):
        return [
            remote(
                buffer.at[k, y],
                buffer.at[k, y],
                ring_send.at[phase, k, i],
                ring_recv.at[phase, k, i],
                peer,
            )
            for i, peer in enumerate(around)
        ]

    def scatter(source, target, phase, k):
        copies = [
            remote(
                source.at[k, peer[1] // 2],
                target.at[k, y],
                ring_send.at[phase, k, i],
                ring_recv.at[phase, k, i],
                peer,
            )
            for i, peer in enumerate(around)
        ]
        target[k, y] = source[k, y]
        return copies

    sent = []

    def drain():
        while sent:
            sent.pop().wait_send()

    def arrive(copies):
        for copy in copies:
            copy.wait_recv()
        sent.extend(copies)

    def gathered(buffer, k):
        return jnp.concatenate([buffer[k, i].astype(F32) for i in range(CHIPS)], axis=0)

    def total(buffer, k):
        out_sum = buffer[k, 0].astype(F32)
        for i in range(1, CHIPS):
            out_sum = out_sum + buffer[k, i].astype(F32)
        return out_sum

    swap = remote(swap_out, normed_all.at[0, y], swap_send.at[0], swap_recv.at[0], beside)
    direct = spread(normed_all, 0, 1)

    def label(i, of, peer):
        return remote(
            window_all.at[of], window_all.at[of], label_send.at[i], label_recv.at[i], peer
        )

    early[1].wait()
    labels = [label(i, t, peer) for i, peer in enumerate([beside] + around)]
    mine, theirs = halves(features)
    kept[1] = mine
    raw_out[...] = theirs.astype(BF16)
    raw = remote(raw_out, raw_in, swap_send.at[1], swap_recv.at[1], beside)
    swap.wait_recv()
    forwarded = spread(normed_all, 0, 0)
    labels[0].wait_recv()
    labels += [label(4 + i, beside[1], peer) for i, peer in enumerate(around)]

    mine_at = pl.multiple_of(c * 160, 16)
    pairs = [(qkv_bias, bias_qkv.at[c]), (fc1_bias, None)]
    for which, start in enumerate((0, HEAD_LANES, HEAD_LANES + 320)):
        pairs.append((qkv_weight.at[which], wqkv.at[pl.ds(start + mine_at, 160)]))
    pairs.append((proj_weight, wproj.at[pl.ds(64 + mine_at, 160)]))
    pairs += [(fc1_weight, wfc1.at[c]), (fc2_weight, wfc2.at[c])]
    pushed, loaded = [], []
    for i, (src, dst) in enumerate(pairs):
        there, here = (fc1_other, fc1_own) if dst is None else (dst, dst)
        pushed.append(remote(src, there, weight_send.at[i], weight_recv.at[i], beside))
        loaded.append(pltpu.make_async_copy(src, here, load_sem.at[i]))
        loaded[-1].start()
    sent += [swap, raw]

    for i in range(2, 6):
        lay_out(i)
    gap = jnp.zeros((64, D), BF16)
    wqkv[320:HEAD_LANES, :] = gap
    wproj[0:64, :] = gap
    early[2].wait()
    own_count = count_all[d]
    for copy in loaded:
        copy.wait()
    for copy in pushed[:2]:
        copy.wait_recv()
    pieces = []
    for which in range(3):
        for core in range(2):
            pieces.append(bias_qkv[core, which : which + 1, :].astype(F32))
        if which == 0:
            pieces.append(jnp.zeros((1, 64), F32))
    wide_bias[...] = jnp.concatenate(pieces, axis=1)
    own_bias = fc1_own[...].astype(F32).reshape(1, 320)
    other_bias = fc1_other[...].astype(F32).reshape(1, 320)
    wide_fc1[...] = jnp.concatenate(
        [jnp.where(c == 0, own_bias, other_bias), jnp.where(c == 0, other_bias, own_bias)], axis=1
    )

    arrive(labels[1:])
    sent.append(labels[0])
    label_rows[...] = jnp.zeros(label_rows.shape, F32)
    for i in range(2 * CHIPS):
        label_rows[8 * i : 8 * i + TOKENS, :] = window_all[i].astype(F32)
    row, col = iotas((2 * GROUP, 16 * CHIPS))
    origin = jnp.where(row < GROUP, other, c)
    source = (row % GROUP // ROWS * 2 + origin) * 8 + row % ROWS // HALF
    spread_labels = matmul(one_hot(col == source), label_rows[...].astype(BF16))
    row, col = iotas((2 * GROUP, SLOTS))
    own_label = jnp.where(col == HALF * c + row % HALF, spread_labels, 0.0)
    own_label = jnp.sum(own_label, axis=1, keepdims=True).astype(jnp.int32)
    row, col = iotas((2 * GROUP, 128))
    marks = one_hot(col == own_label + 4 * (row % HALF))
    same = matmul_t(marks, marks)
    for copy in pushed[2:6]:
        copy.wait_recv()
    sent += pushed[:6]

    arrive(direct)
    arrive(forwarded)
    everything = jnp.concatenate([gathered(normed_all, k) for k in range(2)], axis=0).astype(BF16)
    qkv = (matmul_t(everything, wqkv[...]) + wide_bias[...]).astype(BF16)
    query, keys, values = (
        qkv[:, start : start + HEAD_LANES] for start in (0, HEAD_LANES, HEAD_LANES + 256)
    )
    row, lane = iotas((GROUP, HEAD_LANES))
    scale = 1.0 / (float(HEAD_DIM) ** 0.5)
    summing = []
    for k in range(2):
        part = query[GROUP * k : GROUP * (k + 1)]
        heads = []
        for j in range(HEADS):
            mask = (lane >= HEAD_DIM * j) & (lane < HEAD_DIM * (j + 1))
            heads.append(jnp.where(mask, part, 0.0).astype(BF16))
        scores = matmul_t(jnp.concatenate(heads, axis=0), keys) * scale
        inside = jnp.concatenate([same[GROUP * k : GROUP * (k + 1)] > 0.5] * HEADS, axis=0)
        weights = jnp.where(inside, jnp.exp(scores), 0.0)
        weights = weights / jnp.sum(weights, axis=1, keepdims=True)
        mixture = matmul(weights.astype(BF16), values)
        attended = jnp.zeros((GROUP, HEAD_LANES), F32)
        for j in range(HEADS):
            mask = (lane >= 64 + HEAD_DIM * j) & (lane < 64 + HEAD_DIM * (j + 1))
            attended = jnp.where(mask, mixture[GROUP * j : GROUP * (j + 1)], attended)
        mixed_part = matmul(attended.astype(BF16), wproj[...])
        part_out[k] = mixed_part.reshape(CHIPS, ROWS, D).astype(BF16)
        summing.append(scatter(part_out, part_in, 1, k))

    raw.wait_recv()
    kept[0] = raw_in[...].astype(F32)
    drain()
    moving = []
    for k in range(2):
        arrive(summing[k])
        mixed = (total(part_in, k) + vector(2) + kept[k]).astype(BF16).astype(F32)
        kept[k] = mixed + vector(5)
        normed2_all[k, y] = normalize(mixed, vector(3), vector(4)).astype(BF16)
        moving.append(spread(normed2_all, 2, k))

    for copy in pushed[6:]:
        copy.wait_recv()
    sent += pushed[6:]
    drain()
    summing = []
    for k in range(2):
        arrive(moving[k])
        activations = gathered(normed2_all, k).astype(BF16)
        lifted = matmul_t(activations, wfc1[...].reshape(640, D)) + wide_fc1[...]
        hidden = (lifted * jax.nn.sigmoid(1.702 * lifted)).astype(BF16)
        ffn_part = matmul(hidden, wfc2[...].reshape(640, D))
        ffn_out[k] = ffn_part.reshape(CHIPS, ROWS, D).astype(BF16)
        summing.append(scatter(ffn_out, ffn_in, 3, k))

    drain()
    row, col = iotas((ROWS, D))
    live = HALF * c + row % HALF < own_count
    arrive(summing[0])
    done_out[...] = jnp.where(live, total(ffn_in, 0) + kept[0], 0.0).astype(BF16)
    back = remote(done_out, done_in, swap_send.at[2], swap_recv.at[2], beside)
    arrive(summing[1])
    mine = jnp.where(live, total(ffn_in, 1) + kept[1], 0.0)
    arrive([back])
    theirs = done_in[...].astype(F32)
    low, high = jnp.where(c == 0, mine, theirs), jnp.where(c == 0, theirs, mine)
    for i in range(TOKENS):
        rows = [part[HALF * i : HALF * (i + 1)] for part in (low, high)]
        out[i] = jnp.concatenate(rows, axis=0).astype(BF16)
    drain()


def on_device(
    tiles,
    window_ids,
    counts,
    ln_gain,
    ln_bias,
    qkv_weight,
    qkv_bias,
    proj_weight,
    proj_bias,
    mlp_gain,
    mlp_bias,
    fc1_weight,
    fc1_bias,
    fc2_weight,
    fc2_bias,
):
    operands = (
        counts,
        jnp.transpose(window_ids),
        jnp.transpose(tiles, (1, 0, 2)),
        ln_gain,
        ln_bias,
        jnp.swapaxes(qkv_weight, 1, 2),
        qkv_bias,
        proj_weight,
        proj_bias,
        mlp_gain,
        mlp_bias,
        jnp.transpose(fc1_weight),
        fc1_bias,
        fc2_weight,
        fc2_bias,
    )
    encoded = pl.pallas_call(
        encode,
        out_shape=pltpu.VMEM((TOKENS, SLOTS, D), BF16),
        in_specs=[pl.BlockSpec(memory_space=pltpu.HBM)] * len(operands),
        out_specs=pl.BlockSpec(memory_space=pltpu.VMEM),
        scratch_shapes=[
            pltpu.SMEM((64,), jnp.int32),
            pltpu.VMEM((2 * CHIPS, TOKENS, SLOTS), jnp.int32),
            pltpu.VMEM((16 * CHIPS, SLOTS), F32),
            [pltpu.VMEM((D,), BF16)] * 6,
            pltpu.VMEM((2, 3, 160), BF16),
            pltpu.VMEM((320,), BF16),
            pltpu.VMEM((320,), BF16),
            pltpu.VMEM((8, D), F32),
            pltpu.VMEM((1, 1024), F32),
            pltpu.VMEM((1, 640), F32),
            pltpu.VMEM((1024, D), BF16),
            pltpu.VMEM((HEAD_LANES, D), BF16),
            pltpu.VMEM((2, 320, D), BF16),
            pltpu.VMEM((2, 320, D), BF16),
            pltpu.VMEM((TOKENS, SLOTS, D), BF16),
            pltpu.VMEM((ROWS, D), BF16),
            pltpu.VMEM((ROWS, D), BF16),
            pltpu.VMEM((ROWS, D), BF16),
            pltpu.VMEM((2, ROWS, D), F32),
            pltpu.VMEM((2, CHIPS, ROWS, D), BF16),
            pltpu.VMEM((2, CHIPS, ROWS, D), BF16),
            pltpu.VMEM((2, CHIPS, ROWS, D), BF16),
            pltpu.VMEM((2, CHIPS, ROWS, D), BF16),
            pltpu.VMEM((2, CHIPS, ROWS, D), BF16),
            pltpu.VMEM((2, CHIPS, ROWS, D), BF16),
            pltpu.VMEM((ROWS, D), BF16),
            pltpu.VMEM((ROWS, D), BF16),
            pltpu.SemaphoreType.DMA((3,)),
            pltpu.SemaphoreType.DMA((6,)),
            pltpu.SemaphoreType.DMA((8,)),
            pltpu.SemaphoreType.DMA((8,)),
            pltpu.SemaphoreType.DMA((8,)),
            pltpu.SemaphoreType.DMA((7,)),
            pltpu.SemaphoreType.DMA((7,)),
            pltpu.SemaphoreType.DMA((3,)),
            pltpu.SemaphoreType.DMA((3,)),
            pltpu.SemaphoreType.DMA((4, 2, 3)),
            pltpu.SemaphoreType.DMA((4, 2, 3)),
        ],
        compiler_params=pltpu.CompilerParams(
            collective_id=0, has_side_effects=True, vmem_limit_bytes=48 * 2**20
        ),
        name="encode",
    )(*(pltpu.with_memory_space_constraint(operand, pltpu.HBM) for operand in operands))
    return jnp.transpose(encoded, (1, 0, 2))


def solution(mesh):
    placed = (
        P("dp", "tensor", None),
        P("dp", "tensor"),
        P(),
        P(),
        P(),
        P(None, None, "tensor"),
        P(None, "tensor"),
        P("tensor", None),
        P(),
        P(),
        P(),
        P(None, "tensor"),
        P("tensor"),
        P("tensor", None),
        P(),
    )
    return jax.shard_map(
        on_device, mesh=mesh, in_specs=placed, out_specs=P("dp", "tensor", None), check_vma=False
    )
```

```python
import jax
import jax.numpy as jnp
from jax import lax
from jax.experimental import pallas as pl
from jax.experimental.pallas import tpu as pltpu
from jax.sharding import PartitionSpec as P

D = 1280
HEAD_DIM = 80
CHIPS = 4
SLOTS = 16
HALF = SLOTS // 2
TOKENS = 3
ROWS = TOKENS * HALF
GROUP = CHIPS * ROWS
HEADS = 4
HEAD_LANES = 384
MESH = pl.DeviceIdType.MESH
F32 = jnp.float32
BF16 = jnp.bfloat16


def matmul(left, right):
    return jnp.dot(left, right, preferred_element_type=F32)


def matmul_t(left, right):
    return lax.dot_general(left, right, (((1,), (1,)), ((), ())), preferred_element_type=F32)


def normalize(rows, gain, shift):
    centred = rows - jnp.mean(rows, axis=-1, keepdims=True)
    variance = jnp.mean(centred * centred, axis=-1, keepdims=True)
    return centred * lax.rsqrt(variance + 1e-06) * gain + shift


def iotas(shape):
    return (
        lax.broadcasted_iota(jnp.int32, shape, 0),
        lax.broadcasted_iota(jnp.int32, shape, 1),
    )


def one_hot(flags):
    return jnp.where(flags, 1.0, 0.0).astype(BF16)


def encode(
    counts,
    window,
    tiles,
    ln_gain,
    ln_bias,
    qkv_weight,
    qkv_bias,
    proj_weight,
    proj_bias,
    mlp_gain,
    mlp_bias,
    fc1_weight,
    fc1_bias,
    fc2_weight,
    fc2_bias,
    out,
    count_all,
    window_all,
    label_rows,
    shifts,
    bias_qkv,
    fc1_own,
    fc1_other,
    vec,
    wide_bias,
    wide_fc1,
    wqkv,
    wproj,
    wfc1,
    wfc2,
    wqkv_t,
    wfc1_t,
    tile_rows,
    swap_out,
    raw_out,
    raw_in,
    kept,
    normed_all,
    part_out,
    part_in,
    normed2_all,
    ffn_out,
    ffn_in,
    done_out,
    done_in,
    early_sem,
    plain_sem,
    load_sem,
    weight_send,
    weight_recv,
    label_send,
    label_recv,
    swap_send,
    swap_recv,
    ring_send,
    ring_recv,
):
    d, t = lax.axis_index("dp"), lax.axis_index("tensor")
    y, c = t // 2, t % 2
    other = 1 - c
    beside = (d, y * 2 + other)
    around = [(d, ((y + k) % CHIPS) * 2 + c) for k in (2, 1, 3)]

    barrier = pltpu.get_barrier_semaphore()
    for peer in around + [beside]:
        pl.semaphore_signal(barrier, inc=1, device_id=peer, device_id_type=MESH)

    early = []
    for i, (src, dst) in enumerate(
        ((tiles, tile_rows), (window, window_all.at[t]), (counts, count_all))
    ):
        early.append(pltpu.make_async_copy(src, dst, early_sem.at[i]))
        early[-1].start()
    plain = []
    for i, src in enumerate((ln_gain, ln_bias, proj_bias, mlp_gain, mlp_bias, fc2_bias)):
        plain.append(pltpu.make_async_copy(src, shifts[i], plain_sem.at[i]))
        plain[-1].start()

    def vector(i):
        return vec[i : i + 1, :]

    def lay_out(i):
        plain[i].wait()
        vec[i : i + 1, :] = shifts[i][...].astype(F32).reshape(1, D)

    def halves(rows):
        low = [rows[SLOTS * i : SLOTS * i + HALF] for i in range(TOKENS)]
        high = [rows[SLOTS * i + HALF : SLOTS * (i + 1)] for i in range(TOKENS)]
        low, high = jnp.concatenate(low, axis=0), jnp.concatenate(high, axis=0)
        return jnp.where(c == 0, low, high), jnp.where(c == 0, high, low)

    lay_out(0)
    lay_out(1)
    early[0].wait()
    features = tile_rows[...].astype(F32).reshape(TOKENS * SLOTS, D)
    mine, theirs = halves(normalize(features, vector(0), vector(1)))
    swap_out[...] = theirs.astype(BF16)
    normed_all[1, y] = mine.astype(BF16)

    pl.semaphore_wait(barrier, len(around) + 1)

    def remote(src, dst, send, recv, peer):
        copy = pltpu.make_async_remote_copy(
            src_ref=src,
            dst_ref=dst,
            send_sem=send,
            recv_sem=recv,
            device_id=peer,
            device_id_type=MESH,
        )
        copy.start()
        return copy

    def spread(buffer, phase, k):
        return [
            remote(
                buffer.at[k, y],
                buffer.at[k, y],
                ring_send.at[phase, k, i],
                ring_recv.at[phase, k, i],
                peer,
            )
            for i, peer in enumerate(around)
        ]

    def scatter(source, target, phase, k):
        copies = [
            remote(
                source.at[k, peer[1] // 2],
                target.at[k, y],
                ring_send.at[phase, k, i],
                ring_recv.at[phase, k, i],
                peer,
            )
            for i, peer in enumerate(around)
        ]
        target[k, y] = source[k, y]
        return copies

    sent = []

    def drain():
        while sent:
            sent.pop().wait_send()

    def arrive(copies):
        for copy in copies:
            copy.wait_recv()
        sent.extend(copies)

    def gathered(buffer, k):
        return jnp.concatenate([buffer[k, i].astype(F32) for i in range(CHIPS)], axis=0)

    def total(buffer, k):
        out_sum = buffer[k, 0].astype(F32)
        for i in range(1, CHIPS):
            out_sum = out_sum + buffer[k, i].astype(F32)
        return out_sum

    def label(i, of, peer):
        return remote(
            window_all.at[of], window_all.at[of], label_send.at[i], label_recv.at[i], peer
        )

    early[1].wait()
    labels = [label(0, t, beside)]
    swap = remote(swap_out, normed_all.at[0, y], swap_send.at[0], swap_recv.at[0], beside)
    labels += [label(1 + i, t, peer) for i, peer in enumerate(around)]
    direct = spread(normed_all, 0, 1)
    mine, theirs = halves(features)
    kept[1] = mine
    raw_out[...] = theirs.astype(BF16)
    raw = remote(raw_out, raw_in, swap_send.at[1], swap_recv.at[1], beside)
    labels[0].wait_recv()
    labels += [label(4 + i, beside[1], peer) for i, peer in enumerate(around)]
    swap.wait_recv()
    forwarded = spread(normed_all, 0, 0)

    mine_at = pl.multiple_of(c * 160, 16)
    pairs = [(qkv_bias, bias_qkv.at[c]), (fc1_bias, None)]
    for which, start in enumerate((0, HEAD_LANES, HEAD_LANES + 320)):
        pairs.append((qkv_weight.at[which], wqkv.at[pl.ds(start + mine_at, 160)]))
    pairs.append((proj_weight, wproj.at[pl.ds(64 + mine_at, 160)]))
    pairs += [(fc1_weight, wfc1.at[c]), (fc2_weight, wfc2.at[c])]
    pushed, loaded = [], []
    for i, (src, dst) in enumerate(pairs):
        there, here = (fc1_other, fc1_own) if dst is None else (dst, dst)
        pushed.append(remote(src, there, weight_send.at[i], weight_recv.at[i], beside))
        loaded.append(pltpu.make_async_copy(src, here, load_sem.at[i]))
        loaded[-1].start()
    sent += [swap, raw]

    for i in range(2, 6):
        lay_out(i)
    gap = jnp.zeros((64, D), BF16)
    wqkv[320:HEAD_LANES, :] = gap
    wproj[0:64, :] = gap
    early[2].wait()
    own_count = count_all[d]
    for copy in loaded:
        copy.wait()
    for copy in pushed[:2]:
        copy.wait_recv()
    pieces = []
    for which in range(3):
        for core in range(2):
            pieces.append(bias_qkv[core, which : which + 1, :].astype(F32))
        if which == 0:
            pieces.append(jnp.zeros((1, 64), F32))
    wide_bias[...] = jnp.concatenate(pieces, axis=1)
    own_bias = fc1_own[...].astype(F32).reshape(1, 320)
    other_bias = fc1_other[...].astype(F32).reshape(1, 320)
    wide_fc1[...] = jnp.concatenate(
        [jnp.where(c == 0, own_bias, other_bias), jnp.where(c == 0, other_bias, own_bias)], axis=1
    )

    for copy in pushed[2:6]:
        copy.wait_recv()
    sent += pushed[:6]
    wqkv_t[...] = wqkv[...].T

    qkv = [None, None]
    for k, copies in ((1, direct), (0, forwarded)):
        arrive(copies)
        rows = gathered(normed_all, k).astype(BF16)
        qkv[k] = (matmul(rows, wqkv_t[...]) + wide_bias[...]).astype(BF16)
        if k == 1:
            arrive(labels[1:])
            sent.append(labels[0])
            label_rows[...] = jnp.zeros(label_rows.shape, F32)
            for i in range(2 * CHIPS):
                label_rows[8 * i : 8 * i + TOKENS, :] = window_all[i].astype(F32)
            row, col = iotas((2 * GROUP, 16 * CHIPS))
            origin = jnp.where(row < GROUP, other, c)
            source = (row % GROUP // ROWS * 2 + origin) * 8 + row % ROWS // HALF
            spread_labels = matmul(one_hot(col == source), label_rows[...].astype(BF16))
            row, col = iotas((2 * GROUP, SLOTS))
            own_label = jnp.where(col == HALF * c + row % HALF, spread_labels, 0.0)
            own_label = jnp.sum(own_label, axis=1, keepdims=True).astype(jnp.int32)
            row, col = iotas((2 * GROUP, 128))
            marks = one_hot(col == own_label + 4 * (row % HALF))
            same = matmul_t(marks, marks)
    keys = jnp.concatenate([part[:, HEAD_LANES : 2 * HEAD_LANES] for part in qkv], axis=0)
    values = jnp.concatenate([part[:, HEAD_LANES + 256 :] for part in qkv], axis=0)
    row, lane = iotas((GROUP, HEAD_LANES))
    scale = 1.0 / (float(HEAD_DIM) ** 0.5)
    summing = []
    for k in range(2):
        part = qkv[k][:, :HEAD_LANES]
        heads = []
        for j in range(HEADS):
            mask = (lane >= HEAD_DIM * j) & (lane < HEAD_DIM * (j + 1))
            heads.append(jnp.where(mask, part, 0.0).astype(BF16))
        scores = matmul_t(jnp.concatenate(heads, axis=0), keys) * scale
        inside = jnp.concatenate([same[GROUP * k : GROUP * (k + 1)] > 0.5] * HEADS, axis=0)
        weights = jnp.where(inside, jnp.exp(scores), 0.0)
        weights = weights / jnp.sum(weights, axis=1, keepdims=True)
        mixture = matmul(weights.astype(BF16), values)
        attended = jnp.zeros((GROUP, HEAD_LANES), F32)
        for j in range(HEADS):
            mask = (lane >= 64 + HEAD_DIM * j) & (lane < 64 + HEAD_DIM * (j + 1))
            attended = jnp.where(mask, mixture[GROUP * j : GROUP * (j + 1)], attended)
        mixed_part = matmul(attended.astype(BF16), wproj[...])
        part_out[k] = mixed_part.reshape(CHIPS, ROWS, D).astype(BF16)
        summing.append(scatter(part_out, part_in, 1, k))

    for copy in pushed[6:]:
        copy.wait_recv()
    sent += pushed[6:]
    wfc1_t[...] = wfc1[...].reshape(640, D).T
    raw.wait_recv()
    kept[0] = raw_in[...].astype(F32)
    drain()
    moving = []
    for k in range(2):
        arrive(summing[k])
        mixed = (total(part_in, k) + vector(2) + kept[k]).astype(BF16).astype(F32)
        kept[k] = mixed + vector(5)
        normed2_all[k, y] = normalize(mixed, vector(3), vector(4)).astype(BF16)
        moving.append(spread(normed2_all, 2, k))

    drain()
    summing = []
    for k in range(2):
        arrive(moving[k])
        activations = gathered(normed2_all, k).astype(BF16)
        lifted = matmul(activations, wfc1_t[...]) + wide_fc1[...]
        hidden = (lifted * jax.nn.sigmoid(1.702 * lifted)).astype(BF16)
        ffn_part = matmul(hidden, wfc2[...].reshape(640, D))
        ffn_out[k] = ffn_part.reshape(CHIPS, ROWS, D).astype(BF16)
        summing.append(scatter(ffn_out, ffn_in, 3, k))

    drain()
    row, col = iotas((ROWS, D))
    live = HALF * c + row % HALF < own_count
    arrive(summing[0])
    done_out[...] = jnp.where(live, total(ffn_in, 0) + kept[0], 0.0).astype(BF16)
    back = remote(done_out, done_in, swap_send.at[2], swap_recv.at[2], beside)
    arrive(summing[1])
    mine = jnp.where(live, total(ffn_in, 1) + kept[1], 0.0)
    arrive([back])
    theirs = done_in[...].astype(F32)
    low, high = jnp.where(c == 0, mine, theirs), jnp.where(c == 0, theirs, mine)
    for i in range(TOKENS):
        rows = [part[HALF * i : HALF * (i + 1)] for part in (low, high)]
        out[i] = jnp.concatenate(rows, axis=0).astype(BF16)
    drain()


def on_device(
    tiles,
    window_ids,
    counts,
    ln_gain,
    ln_bias,
    qkv_weight,
    qkv_bias,
    proj_weight,
    proj_bias,
    mlp_gain,
    mlp_bias,
    fc1_weight,
    fc1_bias,
    fc2_weight,
    fc2_bias,
):
    operands = (
        counts,
        jnp.transpose(window_ids),
        jnp.transpose(tiles, (1, 0, 2)),
        ln_gain,
        ln_bias,
        jnp.swapaxes(qkv_weight, 1, 2),
        qkv_bias,
        proj_weight,
        proj_bias,
        mlp_gain,
        mlp_bias,
        jnp.transpose(fc1_weight),
        fc1_bias,
        fc2_weight,
        fc2_bias,
    )
    encoded = pl.pallas_call(
        encode,
        out_shape=pltpu.VMEM((TOKENS, SLOTS, D), BF16),
        in_specs=[pl.BlockSpec(memory_space=pltpu.HBM)] * len(operands),
        out_specs=pl.BlockSpec(memory_space=pltpu.VMEM),
        scratch_shapes=[
            pltpu.SMEM((64,), jnp.int32),
            pltpu.VMEM((2 * CHIPS, TOKENS, SLOTS), jnp.int32),
            pltpu.VMEM((16 * CHIPS, SLOTS), F32),
            [pltpu.VMEM((D,), BF16)] * 6,
            pltpu.VMEM((2, 3, 160), BF16),
            pltpu.VMEM((320,), BF16),
            pltpu.VMEM((320,), BF16),
            pltpu.VMEM((8, D), F32),
            pltpu.VMEM((1, 1024), F32),
            pltpu.VMEM((1, 640), F32),
            pltpu.VMEM((1024, D), BF16),
            pltpu.VMEM((HEAD_LANES, D), BF16),
            pltpu.VMEM((2, 320, D), BF16),
            pltpu.VMEM((2, 320, D), BF16),
            pltpu.VMEM((D, 1024), BF16),
            pltpu.VMEM((D, 640), BF16),
            pltpu.VMEM((TOKENS, SLOTS, D), BF16),
            pltpu.VMEM((ROWS, D), BF16),
            pltpu.VMEM((ROWS, D), BF16),
            pltpu.VMEM((ROWS, D), BF16),
            pltpu.VMEM((2, ROWS, D), F32),
            pltpu.VMEM((2, CHIPS, ROWS, D), BF16),
            pltpu.VMEM((2, CHIPS, ROWS, D), BF16),
            pltpu.VMEM((2, CHIPS, ROWS, D), BF16),
            pltpu.VMEM((2, CHIPS, ROWS, D), BF16),
            pltpu.VMEM((2, CHIPS, ROWS, D), BF16),
            pltpu.VMEM((2, CHIPS, ROWS, D), BF16),
            pltpu.VMEM((ROWS, D), BF16),
            pltpu.VMEM((ROWS, D), BF16),
            pltpu.SemaphoreType.DMA((3,)),
            pltpu.SemaphoreType.DMA((6,)),
            pltpu.SemaphoreType.DMA((8,)),
            pltpu.SemaphoreType.DMA((8,)),
            pltpu.SemaphoreType.DMA((8,)),
            pltpu.SemaphoreType.DMA((7,)),
            pltpu.SemaphoreType.DMA((7,)),
            pltpu.SemaphoreType.DMA((3,)),
            pltpu.SemaphoreType.DMA((3,)),
            pltpu.SemaphoreType.DMA((4, 2, 3)),
            pltpu.SemaphoreType.DMA((4, 2, 3)),
        ],
        compiler_params=pltpu.CompilerParams(
            collective_id=0, has_side_effects=True, vmem_limit_bytes=48 * 2**20
        ),
        name="encode",
    )(*(pltpu.with_memory_space_constraint(operand, pltpu.HBM) for operand in operands))
    return jnp.transpose(encoded, (1, 0, 2))


def solution(mesh):
    placed = (
        P("dp", "tensor", None),
        P("dp", "tensor"),
        P(),
        P(),
        P(),
        P(None, None, "tensor"),
        P(None, "tensor"),
        P("tensor", None),
        P(),
        P(),
        P(),
        P(None, "tensor"),
        P("tensor"),
        P("tensor", None),
        P(),
    )
    return jax.shard_map(
        on_device, mesh=mesh, in_specs=placed, out_specs=P("dp", "tensor", None), check_vma=False
    )
```

```python
import jax
import jax.numpy as jnp
from jax import lax
from jax.experimental import pallas as pl
from jax.experimental.pallas import tpu as pltpu
from jax.sharding import PartitionSpec as P

D = 1280
HEAD_DIM = 80
CHIPS = 4
SLOTS = 16
HALF = SLOTS // 2
TOKENS = 3
ROWS = TOKENS * HALF
GROUP = CHIPS * ROWS
HEADS = 4
HEAD_LANES = 384
MESH = pl.DeviceIdType.MESH
F32 = jnp.float32
BF16 = jnp.bfloat16


def matmul(left, right):
    return jnp.dot(left, right, preferred_element_type=F32)


def matmul_t(left, right):
    return lax.dot_general(left, right, (((1,), (1,)), ((), ())), preferred_element_type=F32)


def normalize(rows, gain, shift):
    centred = rows - jnp.mean(rows, axis=-1, keepdims=True)
    variance = jnp.mean(centred * centred, axis=-1, keepdims=True)
    return centred * lax.rsqrt(variance + 1e-06) * gain + shift


def iotas(shape):
    return (
        lax.broadcasted_iota(jnp.int32, shape, 0),
        lax.broadcasted_iota(jnp.int32, shape, 1),
    )


def one_hot(flags):
    return jnp.where(flags, 1.0, 0.0).astype(BF16)


def encode(
    counts,
    window,
    tiles,
    ln_gain,
    ln_bias,
    qkv_weight,
    qkv_bias,
    proj_weight,
    proj_bias,
    mlp_gain,
    mlp_bias,
    fc1_weight,
    fc1_bias,
    fc2_weight,
    fc2_bias,
    out,
    count_all,
    window_all,
    label_rows,
    shifts,
    bias_qkv,
    fc1_own,
    fc1_other,
    vec,
    wide_bias,
    wide_fc1,
    wqkv,
    wproj,
    wfc1,
    wfc2,
    wqkv_t,
    wfc1_t,
    tile_rows,
    swap_out,
    raw_out,
    raw_in,
    kept,
    normed_all,
    part_out,
    part_in,
    normed2_all,
    ffn_out,
    ffn_in,
    done_out,
    done_in,
    early_sem,
    plain_sem,
    load_sem,
    weight_send,
    weight_recv,
    label_send,
    label_recv,
    swap_send,
    swap_recv,
    ring_send,
    ring_recv,
):
    d, t = lax.axis_index("dp"), lax.axis_index("tensor")
    y, c = t // 2, t % 2
    other = 1 - c
    beside = (d, y * 2 + other)
    around = [(d, ((y + k) % CHIPS) * 2 + c) for k in (2, 1, 3)]

    barrier = pltpu.get_barrier_semaphore()
    for peer in around + [beside]:
        pl.semaphore_signal(barrier, inc=1, device_id=peer, device_id_type=MESH)

    early = []
    for i, (src, dst) in enumerate(
        ((tiles, tile_rows), (window, window_all.at[t]), (counts, count_all))
    ):
        early.append(pltpu.make_async_copy(src, dst, early_sem.at[i]))
        early[-1].start()
    plain = []
    for i, src in enumerate((ln_gain, ln_bias, proj_bias, mlp_gain, mlp_bias, fc2_bias)):
        plain.append(pltpu.make_async_copy(src, shifts[i], plain_sem.at[i]))
        plain[-1].start()

    def vector(i):
        return vec[i : i + 1, :]

    def lay_out(i):
        plain[i].wait()
        vec[i : i + 1, :] = shifts[i][...].astype(F32).reshape(1, D)

    def halves(rows):
        low = [rows[SLOTS * i : SLOTS * i + HALF] for i in range(TOKENS)]
        high = [rows[SLOTS * i + HALF : SLOTS * (i + 1)] for i in range(TOKENS)]
        low, high = jnp.concatenate(low, axis=0), jnp.concatenate(high, axis=0)
        return jnp.where(c == 0, low, high), jnp.where(c == 0, high, low)

    lay_out(0)
    lay_out(1)
    early[0].wait()
    features = tile_rows[...].astype(F32).reshape(TOKENS * SLOTS, D)
    mine, theirs = halves(normalize(features, vector(0), vector(1)))
    swap_out[...] = theirs.astype(BF16)
    normed_all[1, y] = mine.astype(BF16)

    pl.semaphore_wait(barrier, len(around) + 1)

    def remote(src, dst, send, recv, peer):
        copy = pltpu.make_async_remote_copy(
            src_ref=src,
            dst_ref=dst,
            send_sem=send,
            recv_sem=recv,
            device_id=peer,
            device_id_type=MESH,
        )
        copy.start()
        return copy

    def spread(buffer, phase, k):
        return [
            remote(
                buffer.at[k, y],
                buffer.at[k, y],
                ring_send.at[phase, k, i],
                ring_recv.at[phase, k, i],
                peer,
            )
            for i, peer in enumerate(around)
        ]

    def scatter(source, target, phase, k):
        copies = [
            remote(
                source.at[k, peer[1] // 2],
                target.at[k, y],
                ring_send.at[phase, k, i],
                ring_recv.at[phase, k, i],
                peer,
            )
            for i, peer in enumerate(around)
        ]
        target[k, y] = source[k, y]
        return copies

    sent = []

    def drain():
        while sent:
            sent.pop().wait_send()

    def arrive(copies):
        for copy in copies:
            copy.wait_recv()
        sent.extend(copies)

    def gathered(buffer, k):
        return jnp.concatenate([buffer[k, i].astype(F32) for i in range(CHIPS)], axis=0)

    def total(buffer, k):
        out_sum = buffer[k, 0].astype(F32)
        for i in range(1, CHIPS):
            out_sum = out_sum + buffer[k, i].astype(F32)
        return out_sum

    def label(i, of, peer):
        return remote(
            window_all.at[of], window_all.at[of], label_send.at[i], label_recv.at[i], peer
        )

    early[1].wait()
    labels = [label(0, t, beside)]
    swap = remote(swap_out, normed_all.at[0, y], swap_send.at[0], swap_recv.at[0], beside)
    labels += [label(1 + i, t, peer) for i, peer in enumerate(around)]
    direct = spread(normed_all, 0, 1)
    mine, theirs = halves(features)
    kept[1] = mine
    raw_out[...] = theirs.astype(BF16)
    raw = remote(raw_out, raw_in, swap_send.at[1], swap_recv.at[1], beside)
    labels[0].wait_recv()
    labels += [label(4 + i, beside[1], peer) for i, peer in enumerate(around)]
    swap.wait_recv()
    forwarded = spread(normed_all, 0, 0)

    mine_at = pl.multiple_of(c * 160, 16)
    pairs = [(qkv_bias, bias_qkv.at[c]), (fc1_bias, None)]
    for which, start in enumerate((0, HEAD_LANES, HEAD_LANES + 320)):
        pairs.append((qkv_weight.at[which], wqkv.at[pl.ds(start + mine_at, 160)]))
    pairs.append((proj_weight, wproj.at[pl.ds(64 + mine_at, 160)]))
    pairs += [(fc1_weight, wfc1.at[c]), (fc2_weight, wfc2.at[c])]
    pushed, loaded = [], []
    for i, (src, dst) in enumerate(pairs):
        there, here = (fc1_other, fc1_own) if dst is None else (dst, dst)
        pushed.append(remote(src, there, weight_send.at[i], weight_recv.at[i], beside))
        loaded.append(pltpu.make_async_copy(src, here, load_sem.at[i]))
        loaded[-1].start()
    sent += [swap, raw]

    for i in range(2, 6):
        lay_out(i)
    gap = jnp.zeros((64, D), BF16)
    wqkv[320:HEAD_LANES, :] = gap
    wproj[0:64, :] = gap
    early[2].wait()
    own_count = count_all[d]
    for copy in loaded:
        copy.wait()
    for copy in pushed[:2]:
        copy.wait_recv()
    pieces = []
    for which in range(3):
        for core in range(2):
            pieces.append(bias_qkv[core, which : which + 1, :].astype(F32))
        if which == 0:
            pieces.append(jnp.zeros((1, 64), F32))
    wide_bias[...] = jnp.concatenate(pieces, axis=1)
    own_bias = fc1_own[...].astype(F32).reshape(1, 320)
    other_bias = fc1_other[...].astype(F32).reshape(1, 320)
    wide_fc1[...] = jnp.concatenate(
        [jnp.where(c == 0, own_bias, other_bias), jnp.where(c == 0, other_bias, own_bias)], axis=1
    )

    for copy in pushed[2:6]:
        copy.wait_recv()
    sent += pushed[:6]
    wqkv_t[...] = wqkv[...].T

    qkv = [None, None]
    for k, copies in ((1, direct), (0, forwarded)):
        arrive(copies)
        rows = gathered(normed_all, k).astype(BF16)
        qkv[k] = (matmul(rows, wqkv_t[...]) + wide_bias[...]).astype(BF16)
        if k == 1:
            arrive(labels[1:])
            sent.append(labels[0])
            label_rows[...] = jnp.zeros(label_rows.shape, F32)
            for i in range(2 * CHIPS):
                label_rows[8 * i : 8 * i + TOKENS, :] = window_all[i].astype(F32)
            row, col = iotas((2 * GROUP, 16 * CHIPS))
            origin = jnp.where(row < GROUP, other, c)
            source = (row % GROUP // ROWS * 2 + origin) * 8 + row % ROWS // HALF
            spread_labels = matmul(one_hot(col == source), label_rows[...].astype(BF16))
            row, col = iotas((2 * GROUP, SLOTS))
            own_label = jnp.where(col == HALF * c + row % HALF, spread_labels, 0.0)
            own_label = jnp.sum(own_label, axis=1, keepdims=True).astype(jnp.int32)
            row, col = iotas((2 * GROUP, 128))
            marks = one_hot(col == own_label + 4 * (row % HALF))
            same = matmul_t(marks, marks)
    keys = jnp.concatenate([part[:, HEAD_LANES : 2 * HEAD_LANES] for part in qkv], axis=0)
    values = jnp.concatenate([part[:, HEAD_LANES + 256 :] for part in qkv], axis=0)
    row, lane = iotas((1, HEAD_LANES))
    scale = 1.0 / (float(HEAD_DIM) ** 0.5)
    spans = [(lane >= HEAD_DIM * j) & (lane < HEAD_DIM * (j + 1)) for j in range(HEADS)]
    outs = [
        (lane >= 64 + HEAD_DIM * j) & (lane < 64 + HEAD_DIM * (j + 1)) for j in range(HEADS)
    ]
    spans = [one_hot(span) for span in spans]
    summing = []
    for k in range(2):
        part = qkv[k][:, :HEAD_LANES]
        scores = matmul_t(jnp.concatenate([part * span for span in spans], axis=0), keys)
        inside = same[GROUP * k : GROUP * (k + 1)] > 0.5
        weights = []
        for j in range(HEADS):
            grown = jnp.exp(scores[GROUP * j : GROUP * (j + 1)] * scale)
            grown = jnp.where(inside, grown, 0.0)
            weights.append((grown / jnp.sum(grown, axis=1, keepdims=True)).astype(BF16))
        mixture = matmul(jnp.concatenate(weights, axis=0), values)
        attended = jnp.zeros((GROUP, HEAD_LANES), F32)
        for j in range(HEADS):
            attended = jnp.where(outs[j], mixture[GROUP * j : GROUP * (j + 1)], attended)
        mixed_part = matmul(attended.astype(BF16), wproj[...])
        part_out[k] = mixed_part.reshape(CHIPS, ROWS, D).astype(BF16)
        summing.append(scatter(part_out, part_in, 1, k))

    for copy in pushed[6:]:
        copy.wait_recv()
    sent += pushed[6:]
    wfc1_t[...] = wfc1[...].reshape(640, D).T
    raw.wait_recv()
    kept[0] = raw_in[...].astype(F32)
    drain()
    moving = []
    for k in range(2):
        arrive(summing[k])
        mixed = (total(part_in, k) + vector(2) + kept[k]).astype(BF16).astype(F32)
        kept[k] = mixed + vector(5)
        normed2_all[k, y] = normalize(mixed, vector(3), vector(4)).astype(BF16)
        moving.append(spread(normed2_all, 2, k))

    drain()
    summing = []
    for k in range(2):
        arrive(moving[k])
        activations = gathered(normed2_all, k).astype(BF16)
        lifted = matmul(activations, wfc1_t[...]) + wide_fc1[...]
        hidden = (lifted * jax.nn.sigmoid(1.702 * lifted)).astype(BF16)
        ffn_part = matmul(hidden, wfc2[...].reshape(640, D))
        ffn_out[k] = ffn_part.reshape(CHIPS, ROWS, D).astype(BF16)
        summing.append(scatter(ffn_out, ffn_in, 3, k))

    drain()
    row, col = iotas((ROWS, D))
    live = HALF * c + row % HALF < own_count
    arrive(summing[0])
    done_out[...] = jnp.where(live, total(ffn_in, 0) + kept[0], 0.0).astype(BF16)
    back = remote(done_out, done_in, swap_send.at[2], swap_recv.at[2], beside)
    arrive(summing[1])
    mine = jnp.where(live, total(ffn_in, 1) + kept[1], 0.0)
    arrive([back])
    theirs = done_in[...].astype(F32)
    low, high = jnp.where(c == 0, mine, theirs), jnp.where(c == 0, theirs, mine)
    for i in range(TOKENS):
        rows = [part[HALF * i : HALF * (i + 1)] for part in (low, high)]
        out[i] = jnp.concatenate(rows, axis=0).astype(BF16)
    drain()


def on_device(
    tiles,
    window_ids,
    counts,
    ln_gain,
    ln_bias,
    qkv_weight,
    qkv_bias,
    proj_weight,
    proj_bias,
    mlp_gain,
    mlp_bias,
    fc1_weight,
    fc1_bias,
    fc2_weight,
    fc2_bias,
):
    operands = (
        counts,
        jnp.transpose(window_ids),
        jnp.transpose(tiles, (1, 0, 2)),
        ln_gain,
        ln_bias,
        jnp.swapaxes(qkv_weight, 1, 2),
        qkv_bias,
        proj_weight,
        proj_bias,
        mlp_gain,
        mlp_bias,
        jnp.transpose(fc1_weight),
        fc1_bias,
        fc2_weight,
        fc2_bias,
    )
    encoded = pl.pallas_call(
        encode,
        out_shape=pltpu.VMEM((TOKENS, SLOTS, D), BF16),
        in_specs=[pl.BlockSpec(memory_space=pltpu.HBM)] * len(operands),
        out_specs=pl.BlockSpec(memory_space=pltpu.VMEM),
        scratch_shapes=[
            pltpu.SMEM((64,), jnp.int32),
            pltpu.VMEM((2 * CHIPS, TOKENS, SLOTS), jnp.int32),
            pltpu.VMEM((16 * CHIPS, SLOTS), F32),
            [pltpu.VMEM((D,), BF16)] * 6,
            pltpu.VMEM((2, 3, 160), BF16),
            pltpu.VMEM((320,), BF16),
            pltpu.VMEM((320,), BF16),
            pltpu.VMEM((8, D), F32),
            pltpu.VMEM((1, 1024), F32),
            pltpu.VMEM((1, 640), F32),
            pltpu.VMEM((1024, D), BF16),
            pltpu.VMEM((HEAD_LANES, D), BF16),
            pltpu.VMEM((2, 320, D), BF16),
            pltpu.VMEM((2, 320, D), BF16),
            pltpu.VMEM((D, 1024), BF16),
            pltpu.VMEM((D, 640), BF16),
            pltpu.VMEM((TOKENS, SLOTS, D), BF16),
            pltpu.VMEM((ROWS, D), BF16),
            pltpu.VMEM((ROWS, D), BF16),
            pltpu.VMEM((ROWS, D), BF16),
            pltpu.VMEM((2, ROWS, D), F32),
            pltpu.VMEM((2, CHIPS, ROWS, D), BF16),
            pltpu.VMEM((2, CHIPS, ROWS, D), BF16),
            pltpu.VMEM((2, CHIPS, ROWS, D), BF16),
            pltpu.VMEM((2, CHIPS, ROWS, D), BF16),
            pltpu.VMEM((2, CHIPS, ROWS, D), BF16),
            pltpu.VMEM((2, CHIPS, ROWS, D), BF16),
            pltpu.VMEM((ROWS, D), BF16),
            pltpu.VMEM((ROWS, D), BF16),
            pltpu.SemaphoreType.DMA((3,)),
            pltpu.SemaphoreType.DMA((6,)),
            pltpu.SemaphoreType.DMA((8,)),
            pltpu.SemaphoreType.DMA((8,)),
            pltpu.SemaphoreType.DMA((8,)),
            pltpu.SemaphoreType.DMA((7,)),
            pltpu.SemaphoreType.DMA((7,)),
            pltpu.SemaphoreType.DMA((3,)),
            pltpu.SemaphoreType.DMA((3,)),
            pltpu.SemaphoreType.DMA((4, 2, 3)),
            pltpu.SemaphoreType.DMA((4, 2, 3)),
        ],
        compiler_params=pltpu.CompilerParams(
            collective_id=0, has_side_effects=True, vmem_limit_bytes=48 * 2**20
        ),
        name="encode",
    )(*(pltpu.with_memory_space_constraint(operand, pltpu.HBM) for operand in operands))
    return jnp.transpose(encoded, (1, 0, 2))


def solution(mesh):
    placed = (
        P("dp", "tensor", None),
        P("dp", "tensor"),
        P(),
        P(),
        P(),
        P(None, None, "tensor"),
        P(None, "tensor"),
        P("tensor", None),
        P(),
        P(),
        P(),
        P(None, "tensor"),
        P("tensor"),
        P("tensor", None),
        P(),
    )
    return jax.shard_map(
        on_device, mesh=mesh, in_specs=placed, out_specs=P("dp", "tensor", None), check_vma=False
    )
```

```python
import jax
import jax.numpy as jnp
from jax import lax
from jax.experimental import pallas as pl
from jax.experimental.pallas import tpu as pltpu
from jax.sharding import PartitionSpec as P

D = 1280
HEAD_DIM = 80
CHIPS = 4
SLOTS = 16
HALF = SLOTS // 2
TOKENS = 3
ROWS = TOKENS * HALF
GROUP = CHIPS * ROWS
HEADS = 4
HEAD_LANES = 384
MESH = pl.DeviceIdType.MESH
F32 = jnp.float32
BF16 = jnp.bfloat16


def matmul(left, right):
    return jnp.dot(left, right, preferred_element_type=F32)


def matmul_t(left, right):
    return lax.dot_general(left, right, (((1,), (1,)), ((), ())), preferred_element_type=F32)


def normalize(rows, gain, shift):
    centred = rows - jnp.mean(rows, axis=-1, keepdims=True)
    variance = jnp.mean(centred * centred, axis=-1, keepdims=True)
    return centred * lax.rsqrt(variance + 1e-06) * gain + shift


def iotas(shape):
    return (
        lax.broadcasted_iota(jnp.int32, shape, 0),
        lax.broadcasted_iota(jnp.int32, shape, 1),
    )


def one_hot(flags):
    return jnp.where(flags, 1.0, 0.0).astype(BF16)


def encode(
    counts,
    window,
    tiles,
    ln_gain,
    ln_bias,
    qkv_weight,
    qkv_bias,
    proj_weight,
    proj_bias,
    mlp_gain,
    mlp_bias,
    fc1_weight,
    fc1_bias,
    fc2_weight,
    fc2_bias,
    out,
    count_all,
    window_all,
    label_rows,
    shifts,
    bias_qkv,
    fc1_own,
    fc1_other,
    vec,
    wide_bias,
    wide_fc1,
    wqkv,
    wproj,
    wfc1,
    wfc2,
    wqkv_t,
    wfc1_t,
    tile_rows,
    swap_out,
    raw_out,
    raw_in,
    kept,
    normed_all,
    part_out,
    part_in,
    normed2_all,
    ffn_out,
    ffn_in,
    done_out,
    done_in,
    early_sem,
    plain_sem,
    load_sem,
    weight_send,
    weight_recv,
    label_send,
    label_recv,
    swap_send,
    swap_recv,
    ring_send,
    ring_recv,
):
    d, t = lax.axis_index("dp"), lax.axis_index("tensor")
    y, c = t // 2, t % 2
    other = 1 - c
    beside = (d, y * 2 + other)
    around = [(d, ((y + k) % CHIPS) * 2 + c) for k in (2, 1, 3)]

    barrier = pltpu.get_barrier_semaphore()
    for peer in around + [beside]:
        pl.semaphore_signal(barrier, inc=1, device_id=peer, device_id_type=MESH)

    early = []
    for i, (src, dst) in enumerate(
        ((tiles, tile_rows), (window, window_all.at[t]), (counts, count_all))
    ):
        early.append(pltpu.make_async_copy(src, dst, early_sem.at[i]))
        early[-1].start()
    plain = []
    for i, src in enumerate((ln_gain, ln_bias, proj_bias, mlp_gain, mlp_bias, fc2_bias)):
        plain.append(pltpu.make_async_copy(src, shifts[i], plain_sem.at[i]))
        plain[-1].start()

    def vector(i):
        return vec[i : i + 1, :]

    def lay_out(i):
        plain[i].wait()
        vec[i : i + 1, :] = shifts[i][...].astype(F32).reshape(1, D)

    def halves(rows):
        low = [rows[SLOTS * i : SLOTS * i + HALF] for i in range(TOKENS)]
        high = [rows[SLOTS * i + HALF : SLOTS * (i + 1)] for i in range(TOKENS)]
        low, high = jnp.concatenate(low, axis=0), jnp.concatenate(high, axis=0)
        return jnp.where(c == 0, low, high), jnp.where(c == 0, high, low)

    lay_out(0)
    lay_out(1)
    early[0].wait()
    features = tile_rows[...].astype(F32).reshape(TOKENS * SLOTS, D)
    mine, theirs = halves(normalize(features, vector(0), vector(1)))
    swap_out[...] = theirs.astype(BF16)
    normed_all[1, y] = mine.astype(BF16)

    pl.semaphore_wait(barrier, len(around) + 1)

    def remote(src, dst, send, recv, peer):
        copy = pltpu.make_async_remote_copy(
            src_ref=src,
            dst_ref=dst,
            send_sem=send,
            recv_sem=recv,
            device_id=peer,
            device_id_type=MESH,
        )
        copy.start()
        return copy

    def spread(buffer, phase, k):
        return [
            remote(
                buffer.at[k, y],
                buffer.at[k, y],
                ring_send.at[phase, k, i],
                ring_recv.at[phase, k, i],
                peer,
            )
            for i, peer in enumerate(around)
        ]

    def scatter(source, target, phase, k):
        copies = [
            remote(
                source.at[k, peer[1] // 2],
                target.at[k, y],
                ring_send.at[phase, k, i],
                ring_recv.at[phase, k, i],
                peer,
            )
            for i, peer in enumerate(around)
        ]
        target[k, y] = source[k, y]
        return copies

    sent = []

    def drain():
        while sent:
            sent.pop().wait_send()

    def arrive(copies):
        for copy in copies:
            copy.wait_recv()
        sent.extend(copies)

    def gathered(buffer, k):
        return jnp.concatenate([buffer[k, i].astype(F32) for i in range(CHIPS)], axis=0)

    def total(buffer, k):
        out_sum = buffer[k, 0].astype(F32)
        for i in range(1, CHIPS):
            out_sum = out_sum + buffer[k, i].astype(F32)
        return out_sum

    def label(i, of, peer):
        return remote(
            window_all.at[of], window_all.at[of], label_send.at[i], label_recv.at[i], peer
        )

    early[1].wait()
    labels = [label(0, t, beside)]
    swap = remote(swap_out, normed_all.at[0, y], swap_send.at[0], swap_recv.at[0], beside)
    labels += [label(1 + i, t, peer) for i, peer in enumerate(around)]
    direct = spread(normed_all, 0, 1)
    mine, theirs = halves(features)
    kept[1] = mine
    raw_out[...] = theirs.astype(BF16)
    raw = remote(raw_out, raw_in, swap_send.at[1], swap_recv.at[1], beside)
    labels[0].wait_recv()
    labels += [label(4 + i, beside[1], peer) for i, peer in enumerate(around)]
    swap.wait_recv()
    forwarded = spread(normed_all, 0, 0)

    mine_at = pl.multiple_of(c * 160, 16)
    pairs = [(qkv_bias, bias_qkv.at[c]), (fc1_bias, None)]
    for which, start in enumerate((0, HEAD_LANES, HEAD_LANES + 320)):
        pairs.append((qkv_weight.at[which], wqkv.at[pl.ds(start + mine_at, 160)]))
    pairs.append((proj_weight, wproj.at[pl.ds(64 + mine_at, 160)]))
    pairs += [(fc1_weight, wfc1.at[c]), (fc2_weight, wfc2.at[c])]
    pushed, loaded = [], []
    for i, (src, dst) in enumerate(pairs):
        there, here = (fc1_other, fc1_own) if dst is None else (dst, dst)
        pushed.append(remote(src, there, weight_send.at[i], weight_recv.at[i], beside))
        loaded.append(pltpu.make_async_copy(src, here, load_sem.at[i]))
        loaded[-1].start()
    sent += [swap, raw]

    for i in range(2, 6):
        lay_out(i)
    gap = jnp.zeros((64, D), BF16)
    wqkv[320:HEAD_LANES, :] = gap
    wproj[0:64, :] = gap
    early[2].wait()
    own_count = count_all[d]
    for copy in loaded:
        copy.wait()
    for copy in pushed[:2]:
        copy.wait_recv()
    pieces = []
    for which in range(3):
        for core in range(2):
            pieces.append(bias_qkv[core, which : which + 1, :].astype(F32))
        if which == 0:
            pieces.append(jnp.zeros((1, 64), F32))
    wide_bias[...] = jnp.concatenate(pieces, axis=1)
    own_bias = fc1_own[...].astype(F32).reshape(1, 320)
    other_bias = fc1_other[...].astype(F32).reshape(1, 320)
    wide_fc1[...] = jnp.concatenate(
        [jnp.where(c == 0, own_bias, other_bias), jnp.where(c == 0, other_bias, own_bias)], axis=1
    )

    for copy in pushed[2:6]:
        copy.wait_recv()
    sent += pushed[:6]
    wqkv_t[...] = wqkv[...].T

    qkv = [None, None]
    for k, copies in ((1, direct), (0, forwarded)):
        arrive(copies)
        rows = gathered(normed_all, k).astype(BF16)
        qkv[k] = (matmul(rows, wqkv_t[...]) + wide_bias[...]).astype(BF16)
        if k == 1:
            arrive(labels[1:])
            sent.append(labels[0])
            label_rows[...] = jnp.zeros(label_rows.shape, F32)
            for i in range(2 * CHIPS):
                label_rows[8 * i : 8 * i + TOKENS, :] = window_all[i].astype(F32)
            row, col = iotas((2 * GROUP, 16 * CHIPS))
            origin = jnp.where(row < GROUP, other, c)
            source = (row % GROUP // ROWS * 2 + origin) * 8 + row % ROWS // HALF
            spread_labels = matmul(one_hot(col == source), label_rows[...].astype(BF16))
            row, col = iotas((2 * GROUP, SLOTS))
            own_label = jnp.where(col == HALF * c + row % HALF, spread_labels, 0.0)
            own_label = jnp.sum(own_label, axis=1, keepdims=True).astype(jnp.int32)
            row, col = iotas((2 * GROUP, 128))
            marks = one_hot(col == own_label + 4 * (row % HALF))
            same = matmul_t(marks, marks)
    keys = jnp.concatenate([part[:, HEAD_LANES : 2 * HEAD_LANES] for part in qkv], axis=0)
    values = jnp.concatenate([part[:, HEAD_LANES + 256 :] for part in qkv], axis=0)
    row, lane = iotas((1, HEAD_LANES))
    scale = 1.0 / (float(HEAD_DIM) ** 0.5)
    spans = [(lane >= HEAD_DIM * j) & (lane < HEAD_DIM * (j + 1)) for j in range(HEADS)]
    outs = [
        (lane >= 64 + HEAD_DIM * j) & (lane < 64 + HEAD_DIM * (j + 1)) for j in range(HEADS)
    ]
    spans = [one_hot(span) for span in spans]
    summing = []
    for k in range(2):
        part = qkv[k][:, :HEAD_LANES]
        scores = matmul_t(jnp.concatenate([part * span for span in spans], axis=0), keys)
        inside = same[GROUP * k : GROUP * (k + 1)] > 0.5
        weights = []
        for j in range(HEADS):
            grown = jnp.exp(scores[GROUP * j : GROUP * (j + 1)] * scale)
            grown = jnp.where(inside, grown, 0.0)
            weights.append((grown / jnp.sum(grown, axis=1, keepdims=True)).astype(BF16))
        mixture = matmul(jnp.concatenate(weights, axis=0), values)
        attended = jnp.zeros((GROUP, HEAD_LANES), F32)
        for j in range(HEADS):
            attended = jnp.where(outs[j], mixture[GROUP * j : GROUP * (j + 1)], attended)
        mixed_part = matmul(attended.astype(BF16), wproj[...])
        part_out[k] = mixed_part.reshape(CHIPS, ROWS, D).astype(BF16)
        summing.append(scatter(part_out, part_in, 1, k))
        if k == 0:
            for copy in pushed[6:]:
                copy.wait_recv()
            sent += pushed[6:]
            wfc1_t[...] = wfc1[...].reshape(640, D).T

    raw.wait_recv()
    kept[0] = raw_in[...].astype(F32)
    drain()
    moving = []
    for k in range(2):
        arrive(summing[k])
        mixed = (total(part_in, k) + vector(2) + kept[k]).astype(BF16).astype(F32)
        kept[k] = mixed + vector(5)
        normed2_all[k, y] = normalize(mixed, vector(3), vector(4)).astype(BF16)
        moving.append(spread(normed2_all, 2, k))

    drain()
    summing = []
    for k in range(2):
        arrive(moving[k])
        activations = gathered(normed2_all, k).astype(BF16)
        lifted = matmul(activations, wfc1_t[...]) + wide_fc1[...]
        hidden = (lifted * jax.nn.sigmoid(1.702 * lifted)).astype(BF16)
        ffn_part = matmul(hidden, wfc2[...].reshape(640, D))
        ffn_out[k] = ffn_part.reshape(CHIPS, ROWS, D).astype(BF16)
        summing.append(scatter(ffn_out, ffn_in, 3, k))

    drain()
    row, col = iotas((ROWS, D))
    live = HALF * c + row % HALF < own_count
    arrive(summing[0])
    done_out[...] = jnp.where(live, total(ffn_in, 0) + kept[0], 0.0).astype(BF16)
    back = remote(done_out, done_in, swap_send.at[2], swap_recv.at[2], beside)
    arrive(summing[1])
    mine = jnp.where(live, total(ffn_in, 1) + kept[1], 0.0)
    drain()
    arrive([back])
    theirs = done_in[...].astype(F32)
    low, high = jnp.where(c == 0, mine, theirs), jnp.where(c == 0, theirs, mine)
    for i in range(TOKENS):
        rows = [part[HALF * i : HALF * (i + 1)] for part in (low, high)]
        out[i] = jnp.concatenate(rows, axis=0).astype(BF16)
    drain()


def on_device(
    tiles,
    window_ids,
    counts,
    ln_gain,
    ln_bias,
    qkv_weight,
    qkv_bias,
    proj_weight,
    proj_bias,
    mlp_gain,
    mlp_bias,
    fc1_weight,
    fc1_bias,
    fc2_weight,
    fc2_bias,
):
    operands = (
        counts,
        jnp.transpose(window_ids),
        jnp.transpose(tiles, (1, 0, 2)),
        ln_gain,
        ln_bias,
        jnp.swapaxes(qkv_weight, 1, 2),
        qkv_bias,
        proj_weight,
        proj_bias,
        mlp_gain,
        mlp_bias,
        jnp.transpose(fc1_weight),
        fc1_bias,
        fc2_weight,
        fc2_bias,
    )
    encoded = pl.pallas_call(
        encode,
        out_shape=pltpu.VMEM((TOKENS, SLOTS, D), BF16),
        in_specs=[pl.BlockSpec(memory_space=pltpu.HBM)] * len(operands),
        out_specs=pl.BlockSpec(memory_space=pltpu.VMEM),
        scratch_shapes=[
            pltpu.SMEM((64,), jnp.int32),
            pltpu.VMEM((2 * CHIPS, TOKENS, SLOTS), jnp.int32),
            pltpu.VMEM((16 * CHIPS, SLOTS), F32),
            [pltpu.VMEM((D,), BF16)] * 6,
            pltpu.VMEM((2, 3, 160), BF16),
            pltpu.VMEM((320,), BF16),
            pltpu.VMEM((320,), BF16),
            pltpu.VMEM((8, D), F32),
            pltpu.VMEM((1, 1024), F32),
            pltpu.VMEM((1, 640), F32),
            pltpu.VMEM((1024, D), BF16),
            pltpu.VMEM((HEAD_LANES, D), BF16),
            pltpu.VMEM((2, 320, D), BF16),
            pltpu.VMEM((2, 320, D), BF16),
            pltpu.VMEM((D, 1024), BF16),
            pltpu.VMEM((D, 640), BF16),
            pltpu.VMEM((TOKENS, SLOTS, D), BF16),
            pltpu.VMEM((ROWS, D), BF16),
            pltpu.VMEM((ROWS, D), BF16),
            pltpu.VMEM((ROWS, D), BF16),
            pltpu.VMEM((2, ROWS, D), F32),
            pltpu.VMEM((2, CHIPS, ROWS, D), BF16),
            pltpu.VMEM((2, CHIPS, ROWS, D), BF16),
            pltpu.VMEM((2, CHIPS, ROWS, D), BF16),
            pltpu.VMEM((2, CHIPS, ROWS, D), BF16),
            pltpu.VMEM((2, CHIPS, ROWS, D), BF16),
            pltpu.VMEM((2, CHIPS, ROWS, D), BF16),
            pltpu.VMEM((ROWS, D), BF16),
            pltpu.VMEM((ROWS, D), BF16),
            pltpu.SemaphoreType.DMA((3,)),
            pltpu.SemaphoreType.DMA((6,)),
            pltpu.SemaphoreType.DMA((8,)),
            pltpu.SemaphoreType.DMA((8,)),
            pltpu.SemaphoreType.DMA((8,)),
            pltpu.SemaphoreType.DMA((7,)),
            pltpu.SemaphoreType.DMA((7,)),
            pltpu.SemaphoreType.DMA((3,)),
            pltpu.SemaphoreType.DMA((3,)),
            pltpu.SemaphoreType.DMA((4, 2, 3)),
            pltpu.SemaphoreType.DMA((4, 2, 3)),
        ],
        compiler_params=pltpu.CompilerParams(
            collective_id=0, has_side_effects=True, vmem_limit_bytes=48 * 2**20
        ),
        name="encode",
    )(*(pltpu.with_memory_space_constraint(operand, pltpu.HBM) for operand in operands))
    return jnp.transpose(encoded, (1, 0, 2))


def solution(mesh):
    placed = (
        P("dp", "tensor", None),
        P("dp", "tensor"),
        P(),
        P(),
        P(),
        P(None, None, "tensor"),
        P(None, "tensor"),
        P("tensor", None),
        P(),
        P(),
        P(),
        P(None, "tensor"),
        P("tensor"),
        P("tensor", None),
        P(),
    )
    return jax.shard_map(
        on_device, mesh=mesh, in_specs=placed, out_specs=P("dp", "tensor", None), check_vma=False
    )
```

```python
import jax
import jax.numpy as jnp
from jax import lax
from jax.experimental import pallas as pl
from jax.experimental.pallas import tpu as pltpu
from jax.sharding import PartitionSpec as P

D = 1280
HEAD_DIM = 80
CHIPS = 4
SLOTS = 16
HALF = SLOTS // 2
TOKENS = 3
ROWS = TOKENS * HALF
GROUP = CHIPS * ROWS
HEADS = 4
HEAD_LANES = 384
MESH = pl.DeviceIdType.MESH
F32 = jnp.float32
BF16 = jnp.bfloat16


def matmul(left, right):
    return jnp.dot(left, right, preferred_element_type=F32)


def matmul_t(left, right):
    return lax.dot_general(left, right, (((1,), (1,)), ((), ())), preferred_element_type=F32)


def normalize(rows, gain, shift):
    centred = rows - jnp.mean(rows, axis=-1, keepdims=True)
    variance = jnp.mean(centred * centred, axis=-1, keepdims=True)
    return centred * lax.rsqrt(variance + 1e-06) * gain + shift


def iotas(shape):
    return (
        lax.broadcasted_iota(jnp.int32, shape, 0),
        lax.broadcasted_iota(jnp.int32, shape, 1),
    )


def one_hot(flags):
    return jnp.where(flags, 1.0, 0.0).astype(BF16)


def encode(
    counts,
    window,
    tiles,
    ln_gain,
    ln_bias,
    qkv_weight,
    qkv_bias,
    proj_weight,
    proj_bias,
    mlp_gain,
    mlp_bias,
    fc1_weight,
    fc1_bias,
    fc2_weight,
    fc2_bias,
    out,
    count_all,
    window_all,
    label_rows,
    shifts,
    bias_qkv,
    fc1_own,
    fc1_other,
    vec,
    wide_bias,
    wide_fc1,
    wqkv,
    wproj,
    wfc1,
    wfc2,
    wqkv_t,
    wfc1_t,
    tile_rows,
    swap_out,
    raw_out,
    raw_in,
    kept,
    normed_all,
    part_out,
    part_in,
    normed2_all,
    ffn_out,
    ffn_in,
    done_out,
    done_in,
    early_sem,
    plain_sem,
    load_sem,
    weight_send,
    weight_recv,
    label_send,
    label_recv,
    swap_send,
    swap_recv,
    ring_send,
    ring_recv,
):
    d, t = lax.axis_index("dp"), lax.axis_index("tensor")
    y, c = t // 2, t % 2
    other = 1 - c
    beside = (d, y * 2 + other)
    around = [(d, ((y + k) % CHIPS) * 2 + c) for k in (2, 1, 3)]

    barrier = pltpu.get_barrier_semaphore()
    for peer in around + [beside]:
        pl.semaphore_signal(barrier, inc=1, device_id=peer, device_id_type=MESH)

    early = []
    for i, (src, dst) in enumerate(
        ((tiles, tile_rows), (window, window_all.at[t]), (counts, count_all))
    ):
        early.append(pltpu.make_async_copy(src, dst, early_sem.at[i]))
        early[-1].start()
    plain = []
    for i, src in enumerate((ln_gain, ln_bias, proj_bias, mlp_gain, mlp_bias, fc2_bias)):
        plain.append(pltpu.make_async_copy(src, shifts[i], plain_sem.at[i]))
        plain[-1].start()

    def vector(i):
        return vec[i : i + 1, :]

    def lay_out(i):
        plain[i].wait()
        vec[i : i + 1, :] = shifts[i][...].astype(F32).reshape(1, D)

    def halves(rows):
        low = [rows[SLOTS * i : SLOTS * i + HALF] for i in range(TOKENS)]
        high = [rows[SLOTS * i + HALF : SLOTS * (i + 1)] for i in range(TOKENS)]
        low, high = jnp.concatenate(low, axis=0), jnp.concatenate(high, axis=0)
        return jnp.where(c == 0, low, high), jnp.where(c == 0, high, low)

    lay_out(0)
    lay_out(1)
    early[0].wait()
    features = tile_rows[...].astype(F32).reshape(TOKENS * SLOTS, D)
    mine, theirs = halves(normalize(features, vector(0), vector(1)))
    swap_out[...] = theirs.astype(BF16)
    normed_all[1, y] = mine.astype(BF16)

    pl.semaphore_wait(barrier, len(around) + 1)

    def remote(src, dst, send, recv, peer):
        copy = pltpu.make_async_remote_copy(
            src_ref=src,
            dst_ref=dst,
            send_sem=send,
            recv_sem=recv,
            device_id=peer,
            device_id_type=MESH,
        )
        copy.start()
        return copy

    def spread(buffer, phase, k):
        return [
            remote(
                buffer.at[k, y],
                buffer.at[k, y],
                ring_send.at[phase, k, i],
                ring_recv.at[phase, k, i],
                peer,
            )
            for i, peer in enumerate(around)
        ]

    def scatter(source, target, phase, k):
        copies = [
            remote(
                source.at[k, peer[1] // 2],
                target.at[k, y],
                ring_send.at[phase, k, i],
                ring_recv.at[phase, k, i],
                peer,
            )
            for i, peer in enumerate(around)
        ]
        target[k, y] = source[k, y]
        return copies

    sent = []

    def drain():
        while sent:
            sent.pop().wait_send()

    def arrive(copies):
        for copy in copies:
            copy.wait_recv()
        sent.extend(copies)

    def gathered(buffer, k):
        return jnp.concatenate([buffer[k, i].astype(F32) for i in range(CHIPS)], axis=0)

    def total(buffer, k):
        out_sum = buffer[k, 0].astype(F32)
        for i in range(1, CHIPS):
            out_sum = out_sum + buffer[k, i].astype(F32)
        return out_sum

    def label(i, of, peer):
        return remote(
            window_all.at[of], window_all.at[of], label_send.at[i], label_recv.at[i], peer
        )

    early[1].wait()
    labels = [label(0, t, beside)]
    swap = remote(swap_out, normed_all.at[0, y], swap_send.at[0], swap_recv.at[0], beside)
    labels += [label(1 + i, t, peer) for i, peer in enumerate(around)]
    direct = spread(normed_all, 0, 1)
    mine_at = pl.multiple_of(c * 160, 16)
    pairs = [(qkv_bias, bias_qkv.at[c]), (fc1_bias, None)]
    for which, start in enumerate((0, HEAD_LANES, HEAD_LANES + 320)):
        pairs.append((qkv_weight.at[which], wqkv.at[pl.ds(start + mine_at, 160)]))
    pairs.append((proj_weight, wproj.at[pl.ds(64 + mine_at, 160)]))
    pairs += [(fc1_weight, wfc1.at[c]), (fc2_weight, wfc2.at[c])]
    pushed, loaded = [], []
    def share(i):
        src, dst = pairs[i]
        there, here = (fc1_other, fc1_own) if dst is None else (dst, dst)
        pushed.append(remote(src, there, weight_send.at[i], weight_recv.at[i], beside))
        loaded.append(pltpu.make_async_copy(src, here, load_sem.at[i]))
        loaded[-1].start()

    for i in range(6):
        share(i)
    mine, theirs = halves(features)
    kept[1] = mine
    labels[0].wait_recv()
    labels += [label(4 + i, beside[1], peer) for i, peer in enumerate(around)]
    swap.wait_recv()
    forwarded = spread(normed_all, 0, 0)
    raw_out[...] = theirs.astype(BF16)
    raw = remote(raw_out, raw_in, swap_send.at[1], swap_recv.at[1], beside)

    for i in range(6, len(pairs)):
        share(i)
    sent += [swap, raw]

    for i in range(2, 6):
        lay_out(i)
    gap = jnp.zeros((64, D), BF16)
    wqkv[320:HEAD_LANES, :] = gap
    wproj[0:64, :] = gap
    early[2].wait()
    own_count = count_all[d]
    for copy in loaded:
        copy.wait()
    for copy in pushed[:2]:
        copy.wait_recv()
    pieces = []
    for which in range(3):
        for core in range(2):
            pieces.append(bias_qkv[core, which : which + 1, :].astype(F32))
        if which == 0:
            pieces.append(jnp.zeros((1, 64), F32))
    wide_bias[...] = jnp.concatenate(pieces, axis=1)
    own_bias = fc1_own[...].astype(F32).reshape(1, 320)
    other_bias = fc1_other[...].astype(F32).reshape(1, 320)
    wide_fc1[...] = jnp.concatenate(
        [jnp.where(c == 0, own_bias, other_bias), jnp.where(c == 0, other_bias, own_bias)], axis=1
    )

    for copy in pushed[2:6]:
        copy.wait_recv()
    sent += pushed[:6]
    wqkv_t[...] = wqkv[...].T

    qkv = [None, None]
    for k, copies in ((1, direct), (0, forwarded)):
        arrive(copies)
        rows = gathered(normed_all, k).astype(BF16)
        qkv[k] = (matmul(rows, wqkv_t[...]) + wide_bias[...]).astype(BF16)
        if k == 1:
            arrive(labels[1:])
            sent.append(labels[0])
            label_rows[...] = jnp.zeros(label_rows.shape, F32)
            for i in range(2 * CHIPS):
                label_rows[8 * i : 8 * i + TOKENS, :] = window_all[i].astype(F32)
            row, col = iotas((2 * GROUP, 16 * CHIPS))
            origin = jnp.where(row < GROUP, other, c)
            source = (row % GROUP // ROWS * 2 + origin) * 8 + row % ROWS // HALF
            spread_labels = matmul(one_hot(col == source), label_rows[...].astype(BF16))
            row, col = iotas((2 * GROUP, SLOTS))
            own_label = jnp.where(col == HALF * c + row % HALF, spread_labels, 0.0)
            own_label = jnp.sum(own_label, axis=1, keepdims=True).astype(jnp.int32)
            row, col = iotas((2 * GROUP, 128))
            marks = one_hot(col == own_label + 4 * (row % HALF))
            same = matmul_t(marks, marks)
    keys = jnp.concatenate([part[:, HEAD_LANES : 2 * HEAD_LANES] for part in qkv], axis=0)
    values = jnp.concatenate([part[:, HEAD_LANES + 256 :] for part in qkv], axis=0)
    row, lane = iotas((1, HEAD_LANES))
    scale = 1.0 / (float(HEAD_DIM) ** 0.5)
    spans = [(lane >= HEAD_DIM * j) & (lane < HEAD_DIM * (j + 1)) for j in range(HEADS)]
    outs = [
        (lane >= 64 + HEAD_DIM * j) & (lane < 64 + HEAD_DIM * (j + 1)) for j in range(HEADS)
    ]
    spans = [one_hot(span) for span in spans]
    summing = []
    for k in range(2):
        part = qkv[k][:, :HEAD_LANES]
        scores = matmul_t(jnp.concatenate([part * span for span in spans], axis=0), keys)
        inside = same[GROUP * k : GROUP * (k + 1)] > 0.5
        weights = []
        for j in range(HEADS):
            grown = jnp.exp(scores[GROUP * j : GROUP * (j + 1)] * scale)
            grown = jnp.where(inside, grown, 0.0)
            weights.append((grown / jnp.sum(grown, axis=1, keepdims=True)).astype(BF16))
        mixture = matmul(jnp.concatenate(weights, axis=0), values)
        attended = jnp.zeros((GROUP, HEAD_LANES), F32)
        for j in range(HEADS):
            attended = jnp.where(outs[j], mixture[GROUP * j : GROUP * (j + 1)], attended)
        mixed_part = matmul(attended.astype(BF16), wproj[...])
        part_out[k] = mixed_part.reshape(CHIPS, ROWS, D).astype(BF16)
        summing.append(scatter(part_out, part_in, 1, k))
        if k == 0:
            for copy in pushed[6:]:
                copy.wait_recv()
            sent += pushed[6:]
            wfc1_t[...] = wfc1[...].reshape(640, D).T

    raw.wait_recv()
    kept[0] = raw_in[...].astype(F32)
    drain()
    moving = []
    for k in range(2):
        arrive(summing[k])
        mixed = (total(part_in, k) + vector(2) + kept[k]).astype(BF16).astype(F32)
        kept[k] = mixed + vector(5)
        normed2_all[k, y] = normalize(mixed, vector(3), vector(4)).astype(BF16)
        moving.append(spread(normed2_all, 2, k))

    drain()
    summing = []
    for k in range(2):
        arrive(moving[k])
        activations = gathered(normed2_all, k).astype(BF16)
        lifted = matmul(activations, wfc1_t[...]) + wide_fc1[...]
        hidden = (lifted * jax.nn.sigmoid(1.702 * lifted)).astype(BF16)
        ffn_part = matmul(hidden, wfc2[...].reshape(640, D))
        ffn_out[k] = ffn_part.reshape(CHIPS, ROWS, D).astype(BF16)
        summing.append(scatter(ffn_out, ffn_in, 3, k))

    drain()
    row, col = iotas((ROWS, D))
    live = HALF * c + row % HALF < own_count
    arrive(summing[0])
    done_out[...] = jnp.where(live, total(ffn_in, 0) + kept[0], 0.0).astype(BF16)
    back = remote(done_out, done_in, swap_send.at[2], swap_recv.at[2], beside)
    arrive(summing[1])
    mine = jnp.where(live, total(ffn_in, 1) + kept[1], 0.0)
    drain()
    arrive([back])
    theirs = done_in[...].astype(F32)
    low, high = jnp.where(c == 0, mine, theirs), jnp.where(c == 0, theirs, mine)
    for i in range(TOKENS):
        rows = [part[HALF * i : HALF * (i + 1)] for part in (low, high)]
        out[i] = jnp.concatenate(rows, axis=0).astype(BF16)
    drain()


def on_device(
    tiles,
    window_ids,
    counts,
    ln_gain,
    ln_bias,
    qkv_weight,
    qkv_bias,
    proj_weight,
    proj_bias,
    mlp_gain,
    mlp_bias,
    fc1_weight,
    fc1_bias,
    fc2_weight,
    fc2_bias,
):
    operands = (
        counts,
        jnp.transpose(window_ids),
        jnp.transpose(tiles, (1, 0, 2)),
        ln_gain,
        ln_bias,
        jnp.swapaxes(qkv_weight, 1, 2),
        qkv_bias,
        proj_weight,
        proj_bias,
        mlp_gain,
        mlp_bias,
        jnp.transpose(fc1_weight),
        fc1_bias,
        fc2_weight,
        fc2_bias,
    )
    encoded = pl.pallas_call(
        encode,
        out_shape=pltpu.VMEM((TOKENS, SLOTS, D), BF16),
        in_specs=[pl.BlockSpec(memory_space=pltpu.HBM)] * len(operands),
        out_specs=pl.BlockSpec(memory_space=pltpu.VMEM),
        scratch_shapes=[
            pltpu.SMEM((64,), jnp.int32),
            pltpu.VMEM((2 * CHIPS, TOKENS, SLOTS), jnp.int32),
            pltpu.VMEM((16 * CHIPS, SLOTS), F32),
            [pltpu.VMEM((D,), BF16)] * 6,
            pltpu.VMEM((2, 3, 160), BF16),
            pltpu.VMEM((320,), BF16),
            pltpu.VMEM((320,), BF16),
            pltpu.VMEM((8, D), F32),
            pltpu.VMEM((1, 1024), F32),
            pltpu.VMEM((1, 640), F32),
            pltpu.VMEM((1024, D), BF16),
            pltpu.VMEM((HEAD_LANES, D), BF16),
            pltpu.VMEM((2, 320, D), BF16),
            pltpu.VMEM((2, 320, D), BF16),
            pltpu.VMEM((D, 1024), BF16),
            pltpu.VMEM((D, 640), BF16),
            pltpu.VMEM((TOKENS, SLOTS, D), BF16),
            pltpu.VMEM((ROWS, D), BF16),
            pltpu.VMEM((ROWS, D), BF16),
            pltpu.VMEM((ROWS, D), BF16),
            pltpu.VMEM((2, ROWS, D), F32),
            pltpu.VMEM((2, CHIPS, ROWS, D), BF16),
            pltpu.VMEM((2, CHIPS, ROWS, D), BF16),
            pltpu.VMEM((2, CHIPS, ROWS, D), BF16),
            pltpu.VMEM((2, CHIPS, ROWS, D), BF16),
            pltpu.VMEM((2, CHIPS, ROWS, D), BF16),
            pltpu.VMEM((2, CHIPS, ROWS, D), BF16),
            pltpu.VMEM((ROWS, D), BF16),
            pltpu.VMEM((ROWS, D), BF16),
            pltpu.SemaphoreType.DMA((3,)),
            pltpu.SemaphoreType.DMA((6,)),
            pltpu.SemaphoreType.DMA((8,)),
            pltpu.SemaphoreType.DMA((8,)),
            pltpu.SemaphoreType.DMA((8,)),
            pltpu.SemaphoreType.DMA((7,)),
            pltpu.SemaphoreType.DMA((7,)),
            pltpu.SemaphoreType.DMA((3,)),
            pltpu.SemaphoreType.DMA((3,)),
            pltpu.SemaphoreType.DMA((4, 2, 3)),
            pltpu.SemaphoreType.DMA((4, 2, 3)),
        ],
        compiler_params=pltpu.CompilerParams(
            collective_id=0, has_side_effects=True, vmem_limit_bytes=48 * 2**20
        ),
        name="encode",
    )(*(pltpu.with_memory_space_constraint(operand, pltpu.HBM) for operand in operands))
    return jnp.transpose(encoded, (1, 0, 2))


def solution(mesh):
    placed = (
        P("dp", "tensor", None),
        P("dp", "tensor"),
        P(),
        P(),
        P(),
        P(None, None, "tensor"),
        P(None, "tensor"),
        P("tensor", None),
        P(),
        P(),
        P(),
        P(None, "tensor"),
        P("tensor"),
        P("tensor", None),
        P(),
    )
    return jax.shard_map(
        on_device, mesh=mesh, in_specs=placed, out_specs=P("dp", "tensor", None), check_vma=False
    )
```
